32 devices in a mesh: panel: 8 (over z, x), slab: 4 (over y, core).
Axes of the slice: x: 2, y: 2, z: 4, core: 2. Of those that a mesh axis runs over, the one named last changes fastest.
Arguments:
- charges: bfloat16 [262144], P(('panel', 'slab')), may hold values from -6 to 6
- target: float32 [262144], P(('panel', 'slab')), may hold values from -6 to 6
- stencil: bfloat16 [4096, 64, 256], P(('panel', 'slab')), may hold values from -0.375 to 0.375
- near_matrix: bfloat16 [4096, 4, 4096], P(('panel', 'slab')), may hold values from -0.375 to 0.375
- green: float32 [4096, 4096], P(None, ('panel', 'slab')), may hold values from 0.5 to 8
- block_dest: int32 [4096, 1], P(('panel', 'slab')), may hold values from 0 to 31; in each aligned block of 128 rows (0 to 127, 128 to 255, ...) at most 8 rows name the same one
- block_tile: int32 [4096], P(('panel', 'slab')), may hold values from 0 to 2047
- near_offset: int32 [4096, 4], P(('panel', 'slab')), may hold values from -8 to 8
Outputs:
- potentials: float32 [262144], P(('panel', 'slab'))
- gradient: float32 [262144], P(('panel', 'slab'))
The draws below stay inside these ranges and needn't reach their ends.
Inputs may be any that keep to these rules, and one draw needn't show every extreme that they name: `block_dest`: in the 128 blocks of one device no owner is named more than 8 times; in some device's blocks one owner is named exactly 8 times.
All inputs are finite; a program needn't handle non-finite values.
Results may differ from the reference program's by a relative error of at most 0.0025.
The reference program's roundings to bfloat16 on the way (of `picked` and `residual`) count: a program that leaves them out, or rounds other values in their place, can miss the bound.
Values may be sent and summed in bfloat16 or wider, within the bound.
No kernel may reach another device: no remote copies, remote signals or barrier semaphores. Data moves between devices by JAX's collectives and lax.ppermute only.
A program may use at most 128 MiB of HBM per device.

```python
import math
import jax
import jax.numpy as jnp
import numpy as np
from jax import lax

GRID = 4096
TILE = 16
BLOCK = 64
NEAR = 4
REACH = 8
BLK_DEV = 128
NDEV = 32
CAP = 8
TILE_CELLS = 256
TILES_DEV = 2048
NBLK = 4096
PANELS = 262144


def touch_ends(values, own_key, low, largest):
    longest = values.shape.index(max(values.shape))
    spots = []
    for shift in (0, 1):
        where = [jax.random.randint(jax.random.fold_in(own_key, axis), (), 0, length) for axis, length in enumerate(values.shape)]
        where[longest] = (where[longest] + shift) % values.shape[longest]
        spots.append(tuple(where))
    return values.at[spots[0]].set(low).at[spots[1]].set(largest)


def level_of(rng, shape, split, low, high):
    factor_of, own = 1.0, jax.random.fold_in(rng, 6)
    for position, shards_of in split:
        draws = jnp.exp(jax.random.uniform(jax.random.fold_in(own, position), (shards_of,), jnp.float32, low / len(split), high / len(split)))
        factor_of = factor_of * jnp.repeat(draws, shape[position] // shards_of).reshape([-1 if axis == position else 1 for axis in range(len(shape))])
    return factor_of


def routed_block(key, own, number, rows, number_of, top, limit, lean):
    sequence = jax.random.permutation(key, number_of)
    heavy_load, common = load_shares(number_of, rows * top, limit, lean, True), load_shares(number_of, rows * top, limit, lean, False)
    places = jnp.arange(number_of)

    def named(lengths, offset_by):
        used = int((lengths > 0).sum())
        fixed = max(1, used // 4)
        passed = fixed + (places - fixed + offset_by * (used - fixed)) % max(1, number_of - fixed)
        return jnp.zeros((number_of,), jnp.int32).at[sequence[jnp.where(places < fixed, places, passed)]].set(jnp.asarray(lengths, jnp.int32))

    lengths = jnp.where(number % 4 == 0, named(heavy_load, number // 4), named(common, number - number // 4 - 1))
    mixed = jax.random.permutation(jax.random.fold_in(own, 3), number_of)
    giver, taker = mixed[0:number_of // 2 * 2:2], mixed[1:number_of // 2 * 2:2]
    margin = jnp.minimum(lengths[giver] - 1, limit - lengths[taker]) // 2
    margin = jnp.where((giver == sequence[0]) | (taker == sequence[0]) | (lengths[taker] == 0), 0, jnp.maximum(margin, 0))
    passed = jax.random.randint(jax.random.fold_in(own, 4), (number_of // 2,), 0, 1 << 20) % (margin + 1)
    lengths = lengths.at[giver].add(-passed).at[taker].add(passed)
    items = jnp.searchsorted(jnp.cumsum(lengths), jnp.arange(rows * top), side="right").astype(jnp.int32)
    grid = items.reshape(top, rows).T
    grid = grid[jax.random.permutation(jax.random.fold_in(own, 1), rows)]
    offset_by = jax.random.randint(jax.random.fold_in(own, 2), (rows, 1), 0, top)
    return jnp.take_along_axis(grid, (jnp.arange(top)[None, :] + offset_by) % top, axis=1)


def load_shares(count, total, limit, lean, full):
    portions = [(1 << 20) // math.isqrt(grade ** lean) + 1 for grade in range(1, count + 1)]
    largest = limit if full else min(limit, max(-(-total // count), total * portions[0] // sum(portions)))
    least = 1 if total - largest >= count - 1 else 0
    holding, rest = [largest] + [least] * (count - 1), total - largest - least * (count - 1)
    while rest > 0:
        movable = [i for i in range(1, count) if holding[i] < largest] or [i for i in range(1, count) if holding[i] < limit]
        mass, left = sum([portions[i] for i in movable]), rest
        for i in movable:
            addition = min(limit - holding[i], max(1, left * portions[i] // mass), rest)
            holding[i] = holding[i] + addition
            rest = rest - addition
    return np.array(holding)


def normal_values(key, dims, scale, reach, cuts=(), kind=jnp.bfloat16):
    array = scale * jax.random.normal(key, dims, jnp.float32)
    if cuts:
        array = array * level_of(key, dims, cuts, -0.22, 0.18)
    return jnp.clip(array, -reach, reach).astype(kind)


def setup_inputs(seed: int = 0) -> dict:
    splits = jax.random.split(jax.random.key(seed), 9)
    charges = normal_values(splits[0], (PANELS,), 1.0, 6.0, ((0, 32),))
    target = normal_values(splits[1], (PANELS,), 1.0, 6.0, ((0, 32),), jnp.float32)
    stencil = normal_values(splits[2], (NBLK, BLOCK, TILE_CELLS), TILE_CELLS ** -0.5, 0.375, ((0, 32),))
    near_matrix = normal_values(splits[3], (NBLK, NEAR, BLOCK * BLOCK), (NEAR * BLOCK) ** -0.5, 0.375, ((0, 32),))
    green = jnp.clip(jnp.exp(math.log(8.0) - 2.7725887 * jax.random.uniform(splits[4], (GRID, GRID), jnp.float32) ** level_of(splits[4], (GRID, GRID), ((1, 32),), -0.2, 0.2)), 0.5, 8.0)
    block_dest_keys = jax.random.split(jax.random.fold_in(splits[5], 1), NBLK // BLK_DEV)
    block_dest_turns = jax.random.permutation(jax.random.fold_in(splits[5], 3), NBLK // BLK_DEV)
    block_dest = jax.vmap(lambda own, number: routed_block(jax.random.fold_in(splits[5], 2), own, number, BLK_DEV, NDEV, 1, CAP, 2))(block_dest_keys, block_dest_turns).reshape((NBLK, 1))
    block_tile = touch_ends(jax.random.randint(splits[6], (NBLK,), 0, TILES_DEV), jax.random.fold_in(splits[6], 1), 0, TILES_DEV - 1).astype(jnp.int32)
    near_offset = touch_ends(jax.random.randint(splits[7], (NBLK, NEAR), 0 - REACH, REACH + 1), jax.random.fold_in(splits[7], 1), 0 - REACH, REACH).astype(jnp.int32)
    return {"charges": charges, "target": target, "stencil": stencil, "near_matrix": near_matrix, "green": green, "block_dest": block_dest, "block_tile": block_tile, "near_offset": near_offset}


def reference(charges, target, stencil, near_matrix, green, block_dest, block_tile, near_offset):
    count = NBLK
    sides = GRID // TILE
    weights = stencil.astype(jnp.float32)
    couple = near_matrix.astype(jnp.float32).reshape(count, NEAR, BLOCK, BLOCK)
    global_tile = (block_dest[:, 0] * TILES_DEV + block_tile).astype(jnp.int32)
    positions = (jnp.arange(count, dtype=jnp.int32)[:, None] + REACH + near_offset).astype(jnp.int32)

    def far_field(values):
        tile_values = jnp.einsum('bp,bpt->bt', values.astype(jnp.float32), weights)
        tile_sums = jnp.zeros((sides * sides, TILE_CELLS), jnp.float32).at[global_tile].add(tile_values)
        grid_cells = tile_sums.reshape(sides, sides, TILE, TILE).transpose(0, 2, 1, 3).reshape(GRID, GRID)
        field = jnp.real(jnp.fft.ifft2(green * jnp.fft.fft2(grid_cells)))
        back_tiles = field.reshape(sides, TILE, sides, TILE).transpose(0, 2, 1, 3).reshape(sides * sides, TILE_CELLS)
        picked = back_tiles[global_tile].astype(jnp.bfloat16)
        picked = lax.optimization_barrier(picked).astype(jnp.float32)
        return jnp.einsum('bpt,bt->bp', weights, picked)

    def near_field(values):
        padded = jnp.pad(values.astype(jnp.float32), ((REACH, REACH), (0, 0)))
        return jnp.einsum('bkps,bks->bp', couple, padded[positions])

    def near_adjoint(values):
        terms = jnp.einsum('bkps,bp->bks', couple, values.astype(jnp.float32))
        padded = jnp.zeros((count + 2 * REACH, BLOCK), jnp.float32)
        padded = padded.at[positions.reshape(-1)].add(terms.reshape(-1, BLOCK))
        return padded[REACH:REACH + count]

    charge_blocks = charges.reshape(count, BLOCK)
    potentials = far_field(charge_blocks) + near_field(charge_blocks)
    residual = (potentials - target.reshape(count, BLOCK)).astype(jnp.bfloat16)
    gradient = far_field(residual) + near_adjoint(residual)
    return potentials.reshape(-1), gradient.reshape(-1)
```

```python
import functools
import math

import jax
import jax.numpy as jnp
import numpy as np
from jax import lax
from jax.experimental import pallas as pl
from jax.experimental.pallas import tpu as pltpu
from jax.sharding import PartitionSpec as P

REACH = 8
AXES = ("panel", "slab")
BF16 = jnp.bfloat16
F32 = jnp.float32
VMEM_BYTES = 40 * 1024 * 1024
STEP = 16


def extended_2(cells, sides, width):
    for axis, dim in sides:
        count = lax.axis_size(axis)
        ends = count - 1
        head = lax.slice_in_dim(cells, 0, width, axis=dim)
        tail = lax.slice_in_dim(cells, cells.shape[dim] - width, cells.shape[dim], axis=dim)
        cells = jnp.concatenate(
            [
                lax.ppermute(tail, axis, [(i, (i + 1) % count) for i in range(ends)]),
                cells,
                lax.ppermute(head, axis, [((i + 1) % count, i) for i in range(ends)]),
            ],
            axis=dim,
        )
    return cells


def split(table):
    high = table.astype(jnp.bfloat16)
    return np.stack([high, (table - high.astype(np.float64)).astype(jnp.bfloat16)])


class Plan:
    def __init__(self, grid, tile, devices):
        self.grid, self.tile, self.devices = grid, tile, devices
        self.tile_cols = grid // tile
        self.rows = grid // devices
        self.width = grid // devices
        self.half = self.width // 2
        self.per_mu = devices // tile
        self.kappas = self.tile_cols // 2
        self.group = max(1, min(tile, 2 * 128 // self.rows))

    def place(self, position, mu):
        part, j = divmod(position, self.width)
        device = self.per_mu * mu + part
        if j < self.half:
            return device, j, 1.0
        return self.devices - 1 - device, j - self.half, -1.0

    def kappa(self):
        out = []
        for position in range(self.kappas):
            part, j = divmod(position, self.width)
            if j >= self.half:
                j = self.half + (self.half - (j - self.half)) % self.half
            out.append(self.width * part + j)
        return np.array(out)

    def forward_table(self):
        angle = 2 * np.pi * np.outer(self.kappa(), np.arange(self.tile_cols)) / self.tile_cols
        sine = -np.sin(angle)
        sine[0] = (-1.0) ** np.arange(self.tile_cols)
        return split(np.concatenate([np.cos(angle), sine]))

    def inverse_table(self):
        angle = 2 * np.pi * np.outer(np.arange(self.tile_cols), self.kappa()) / self.tile_cols
        cosine, sine = 2 * np.cos(angle), -2 * np.sin(angle)
        cosine[:, 0] = 1.0
        sine[:, 0] = (-1.0) ** np.arange(self.tile_cols)
        return split(np.concatenate([cosine, sine], axis=1))

    def column_twiddles(self):
        angle = 2 * np.pi * np.outer(np.arange(self.tile), self.kappa()) / self.grid
        full = np.broadcast_to(angle[:, :, None], (self.tile, self.kappas, self.rows))
        return np.cos(full).astype(np.float32), np.sin(full).astype(np.float32)

    def edge_tables(self):
        n, m = self.tile, self.tile // 2
        cells = np.arange(n)
        forward, inverse = np.zeros((2 * n, 2 * n)), np.zeros((2 * n, 2 * n))
        forward[0, :n], forward[n, :n] = 1.0, (-1.0) ** cells
        inverse[:n, 0], inverse[:n, n] = 1.0, (-1.0) ** cells
        for mu in range(1, m):
            angle = 2 * np.pi * cells * mu / n
            forward[mu, :n], forward[n + mu, :n] = np.cos(angle), -np.sin(angle)
            inverse[:n, mu], inverse[:n, n + mu] = 2 * np.cos(angle), -2 * np.sin(angle)
        for nu in range(m):
            angle = 2 * np.pi * cells * (1 + 2 * nu) / (2 * n)
            forward[m + nu, n:], forward[n + m + nu, n:] = np.cos(angle), -np.sin(angle)
            inverse[n:, m + nu], inverse[n:, n + m + nu] = 2 * np.cos(angle), -2 * np.sin(angle)
        return forward.astype(np.float32), inverse.astype(np.float32)

    def spread_table(self):
        n, tile_rows = self.tile, self.rows // self.tile
        eye = np.eye(n)
        table = np.einsum("ai,cj,t->acjti", eye, eye, np.ones(tile_rows))
        return table.reshape(n * n, n * self.rows).astype(jnp.bfloat16)

    def row_tables(self):
        n = self.rows
        angle = 2 * np.pi * (np.outer(np.arange(n), np.arange(n)) % n) / n
        both = split(np.concatenate([np.cos(angle), np.sin(angle)], axis=1))
        angle = 2 * np.pi * np.outer(np.arange(self.devices), np.arange(n)) / self.grid
        angle = angle.reshape(self.devices, 1, n)
        return both, np.cos(angle).astype(np.float32), np.sin(angle).astype(np.float32)

    def mirror_tables(self):
        pick = np.zeros((self.half + STEP, self.width))
        pick[self.half, 0] = 1.0
        for i in range(self.half):
            pick[i, self.width - i if i else self.half] = 1.0
        n = self.rows
        first, rest = np.zeros((n, n)), np.zeros((n, n))
        for i in range(n):
            first[(n - i) % n, i] = 1.0
            rest[n - 1 - i, i] = 1.0
        return pick.astype(jnp.bfloat16), np.stack([first, rest]).astype(jnp.bfloat16)


def transform(points, sign):
    count = len(points)
    if count == 1:
        return points
    even, odd = transform(points[0::2], sign), transform(points[1::2], sign)
    low, high = [], []
    for k in range(count // 2):
        (er, ei), (re, im) = even[k], odd[k]
        if 4 * k == count:
            re, im = (-im, re) if sign > 0 else (im, -re)
        elif 8 * k == count or 8 * k == 3 * count:
            root = math.sqrt(0.5)
            if 8 * k == count:
                re, im = (re - sign * im) * root, (im + sign * re) * root
            else:
                re, im = (-re - sign * im) * root, (sign * re - im) * root
        elif k:
            c, s = math.cos(2 * math.pi * k / count), sign * math.sin(2 * math.pi * k / count)
            re, im = re * c - im * s, im * c + re * s
        low.append((er + re, ei + im))
        high.append((er - re, ei - im))
    return low + high


def dot(a, b):
    return jnp.dot(a, b, preferred_element_type=F32)


def slot_tiles(marks, plan):
    number = marks.astype(jnp.int32) - 1
    shift = plan.tile_cols.bit_length() - 1
    return number & (plan.tile_cols - 1), number >> shift


def slot_mask(tile_row, plan):
    mine = tile_row[:, : plan.rows]
    lane = lax.broadcasted_iota(jnp.int32, mine.shape, 1) // plan.tile
    mask = (mine == lane).astype(F32)
    return jnp.concatenate([mask] * plan.group, axis=1) > 0.5


def forward_rows(plan, values, marks, spread, table, cosine, sine, edge, out, work):
    tile, rows, group, half = plan.tile, plan.rows, plan.group, plan.half
    slots = values.shape[0]
    marks_in = marks[...]
    _, tile_row = slot_tiles(marks_in, plan)
    mask = slot_mask(tile_row, plan)
    tile_col, _ = slot_tiles(marks_in.T[0:1, :], plan)
    place = lax.broadcasted_iota(jnp.int32, (plan.tile_cols, slots), 0)
    chosen = (place == tile_col).astype(F32).astype(BF16)
    weights = dot(table[0], chosen).astype(BF16)
    weights_low = dot(table[1], chosen).astype(BF16)
    exact = values[...]
    high = exact.astype(BF16)
    low = (exact - high.astype(F32)).astype(BF16)
    span = group * rows
    for chunk in range(tile // group):
        lanes = spread[:, chunk * span : (chunk + 1) * span]
        high_part = jnp.where(mask, dot(high, lanes), 0.0).astype(BF16)
        low_part = jnp.where(mask, dot(low, lanes), 0.0).astype(BF16)
        work[chunk] = (
            dot(weights, high_part) + dot(weights, low_part) + dot(weights_low, high_part)
        )

    def piece(cell, start, size):
        at = (cell % group) * rows
        return work[cell // group, start : start + size, at : at + rows]

    ends = [piece(cell, 0, 8)[0:1] for cell in range(tile)]
    ends += [piece(cell, plan.kappas, 8)[0:1] for cell in range(tile)]
    shared = jnp.dot(
        edge[...],
        jnp.concatenate(ends, axis=0),
        precision=lax.Precision.HIGHEST,
        preferred_element_type=F32,
    )
    first = lax.broadcasted_iota(jnp.int32, (STEP, rows), 0) == 0
    for start in range(0, plan.kappas, STEP):
        points = []
        for cell in range(tile):
            re, im = piece(cell, start, STEP), piece(cell, plan.kappas + start, STEP)
            if cell:
                c, s = cosine[cell, start : start + STEP], sine[cell, start : start + STEP]
                re, im = re * c + im * s, im * c - re * s
            points.append((re, im))
        for mu, (re, im) in enumerate(transform(points, -1)):
            if start == 0:
                re = jnp.where(first, shared[mu : mu + 1], re)
                im = jnp.where(first, shared[tile + mu : tile + mu + 1], im)
            device, row, sign = plan.place(start, mu)
            out[device, row : row + STEP] = re.astype(BF16)
            out[device, half + row : half + row + STEP] = (im * sign).astype(BF16)


def inverse_rows(plan, spectrum, marks, spread, table, cosine, sine, edge, out, work):
    tile, rows, group, half = plan.tile, plan.rows, plan.group, plan.half
    slots = marks.shape[0]
    tile_col, tile_row = slot_tiles(marks[...], plan)
    mask = slot_mask(tile_row, plan)
    place = lax.broadcasted_iota(jnp.int32, (slots, plan.tile_cols), 1)
    chosen = (place == tile_col[:, 0:1]).astype(F32).astype(BF16)
    weights = dot(chosen, table[0]).astype(BF16)
    weights_low = dot(chosen, table[1]).astype(BF16)
    ends = [spectrum[plan.per_mu * mu, 0:STEP].astype(F32)[0:1] for mu in range(tile)]
    ends += [spectrum[plan.per_mu * mu, half : half + STEP].astype(F32)[0:1] for mu in range(tile)]
    shared = jnp.dot(
        edge[...],
        jnp.concatenate(ends, axis=0),
        precision=lax.Precision.HIGHEST,
        preferred_element_type=F32,
    )
    first = lax.broadcasted_iota(jnp.int32, (STEP, rows), 0) == 0
    for start in range(0, plan.kappas, STEP):
        points = []
        for mu in range(tile):
            device, row, sign = plan.place(start, mu)
            re = spectrum[device, row : row + STEP].astype(F32)
            im = spectrum[device, half + row : half + row + STEP].astype(F32) * sign
            points.append((re, im))
        for cell, (re, im) in enumerate(transform(points, 1)):
            if cell:
                c, s = cosine[cell, start : start + STEP], sine[cell, start : start + STEP]
                re, im = re * c - im * s, im * c + re * s
            if start == 0:
                re = jnp.where(first, shared[cell : cell + 1], re)
                im = jnp.where(first, shared[tile + cell : tile + cell + 1], im)
            at = (cell % group) * rows
            work[cell // group, start : start + STEP, at : at + rows] = re.astype(BF16)
            work[cell // group, plan.kappas + start : plan.kappas + start + STEP, at : at + rows] = (
                im.astype(BF16)
            )
    span = group * rows
    total = jnp.zeros(out.shape, F32)
    for chunk in range(tile // group):
        field = dot(weights, work[chunk]) + dot(weights_low, work[chunk])
        field = jnp.where(mask, field, 0.0).astype(BF16)
        lanes = spread[:, chunk * span : (chunk + 1) * span]
        total = total + lax.dot_general(
            field, lanes, (((1,), (1,)), ((), ())), preferred_element_type=F32
        )
    out[...] = total.astype(BF16)


def columns(plan, origin, spectrum, green, both, cosine, sine, out, work):
    devices, rows, half = plan.devices, plan.rows, plan.half
    wide = half + 8
    holds_edge = origin[0] == 1
    top = (lax.broadcasted_iota(jnp.int32, (8, rows), 0) == 0) & holds_edge

    def load(s, carry):
        work[s, 0:half] = spectrum[s, 0:half].astype(F32)
        imag = spectrum[s, half : 2 * half].astype(F32)
        work[s, wide : wide + half] = imag
        head = imag[0:8]
        work[s, wide : wide + 8] = jnp.where(top, 0.0, head)
        work[s, half:wide] = jnp.where(top, head, 0.0)
        work[s, wide + half : 2 * wide] = jnp.zeros((8, rows), F32)
        return carry

    lax.fori_loop(0, devices, load, 0)

    def first(g, carry):
        at = pl.multiple_of(g * 8, 8)
        points = [(work[s, pl.ds(at, 8)], work[s, pl.ds(wide + at, 8)]) for s in range(devices)]
        for m, (re, im) in enumerate(transform(points, -1)):
            if m:
                c, s = cosine[m], sine[m]
                re, im = re * c + im * s, im * c - re * s
            work[m, pl.ds(at, 8)] = re
            work[m, pl.ds(wide + at, 8)] = im
        return carry

    lax.fori_loop(0, wide // 8, first, 0)
    batch = 4

    def second(i, carry):
        at = pl.ds(i * batch, batch)
        flat = (batch * 2 * wide, rows)
        y = work[at].reshape(flat).astype(BF16)
        u = (dot(y, both[0]) + dot(y, both[1])).reshape(batch, 2 * wide, 2 * rows)
        g = green[at]
        re = (u[:, :wide, :rows] + u[:, wide:, rows:]) * g
        im = (u[:, wide:, :rows] - u[:, :wide, rows:]) * g
        y = jnp.concatenate([re, im], axis=1).reshape(flat).astype(BF16)
        u = (dot(y, both[0]) + dot(y, both[1])).reshape(batch, 2 * wide, 2 * rows)
        re = u[:, :wide, :rows] - u[:, wide:, rows:]
        im = u[:, wide:, :rows] + u[:, :wide, rows:]
        c, s = cosine[at], sine[at]
        work[at, 0:wide] = re * c - im * s
        work[at, wide : 2 * wide] = im * c + re * s
        return carry

    lax.fori_loop(0, devices // batch, second, 0)

    def third(g, carry):
        at = pl.multiple_of(g * 8, 8)
        points = [(work[m, pl.ds(at, 8)], work[m, pl.ds(wide + at, 8)]) for m in range(devices)]
        for s, (re, im) in enumerate(transform(points, 1)):
            work[s, pl.ds(at, 8)] = re
            work[s, pl.ds(wide + at, 8)] = im
        return carry

    lax.fori_loop(0, wide // 8, third, 0)

    def store(s, carry):
        work[s, wide : wide + 8] = jnp.where(top, work[s, half:wide], work[s, wide : wide + 8])
        out[s, 0:half] = work[s, 0:half].astype(BF16)
        out[s, half : 2 * half] = work[s, wide : wide + half].astype(BF16)
        return carry

    lax.fori_loop(0, devices, store, 0)


def mirrored_green(plan, green, pick, turn, early, late, edge, edge_turned):
    devices, rows, half = plan.devices, plan.rows, plan.half
    for m in range(devices):
        block = green[pl.ds(m, rows, stride=devices), :].astype(BF16)
        picked = lax.dot_general(
            pick[...], block, (((1,), (1,)), ((), ())), preferred_element_type=F32
        )
        turned = dot(picked.astype(BF16), turn[0 if m == 0 else 1])
        mirrored = (devices - m) % devices
        if mirrored < devices // 2:
            early[mirrored] = turned[0:half].astype(BF16)
        else:
            late[mirrored - devices // 2] = turned[0:half].astype(BF16)
        edge[m : m + 1] = picked[half : half + 1]
        edge_turned[mirrored : mirrored + 1] = turned[half : half + 1]


def own_green(plan, follows, green, own):
    devices, rows, half = plan.devices, plan.rows, plan.half
    partner = follows[0] == 1
    first = lax.broadcasted_iota(jnp.int32, (half, rows), 0) == 0
    for m in range(devices):
        turned = green[pl.ds(m, rows, stride=devices), :].T
        swap = jnp.broadcast_to(turned[half : half + 1], (half, rows))
        own[m] = jnp.where(first & partner, swap, turned[0:half])


def kernel(body, plan, out_shape, scratch, scalars, operands):
    in_specs = [pl.BlockSpec(memory_space=pltpu.SMEM)] * len(scalars)
    in_specs += [pl.BlockSpec(memory_space=pltpu.VMEM)] * len(operands)
    return pl.pallas_call(
        functools.partial(body, plan),
        out_shape=out_shape,
        in_specs=in_specs,
        out_specs=jax.tree.map(lambda _: pl.BlockSpec(memory_space=pltpu.VMEM), out_shape),
        scratch_shapes=scratch,
        compiler_params=pltpu.CompilerParams(vmem_limit_bytes=VMEM_BYTES),
    )(*scalars, *operands)


def leaving_green(plan, green):
    devices, half, rows = plan.devices, plan.half, plan.rows
    pick, turn = plan.mirror_tables()
    part = jax.ShapeDtypeStruct((devices // 2, half, rows), BF16)
    line = jax.ShapeDtypeStruct((devices, rows), F32)
    return kernel(
        mirrored_green,
        plan,
        (part, part, line, line),
        [],
        [],
        [green, jnp.asarray(pick), jnp.asarray(turn)],
    )


def staying_green(plan, green):
    devices, half, rows, per_mu = plan.devices, plan.half, plan.rows, plan.per_mu
    partner = lax.axis_index(AXES) % per_mu >= per_mu // 2
    return kernel(
        own_green,
        plan,
        jax.ShapeDtypeStruct((devices, half, rows), F32),
        [],
        [partner.astype(jnp.int32).reshape(1)],
        [green],
    )


def swap_mirrored(plan, part):
    return lax.ppermute(part, AXES, [(i, plan.devices - 1 - i) for i in range(plan.devices)])


def swap_edges(plan, edge, edge_turned):
    devices, per_mu, tile = plan.devices, plan.per_mu, plan.tile
    upper = range(tile // 2, tile)
    plain = [(devices // 2, 0)]
    plain += [(per_mu * (m - tile // 2) + per_mu // 2, per_mu * m) for m in upper]
    mirror = [(devices // 2, 0)]
    mirror += [(per_mu * (tile - 1 - m + tile // 2) + per_mu // 2, per_mu * m) for m in upper]
    for i in range(1, devices):
        low = i % per_mu
        if low < per_mu // 2 and (low or i // per_mu < tile // 2):
            mirror.append((devices - i, i))
    return lax.ppermute(edge, AXES, plain), lax.ppermute(edge_turned, AXES, mirror)


def symmetric_green(plan, own, received, edges, swapped_edges):
    devices, rows, per_mu = plan.devices, plan.rows, plan.per_mu
    tile, grid = plan.tile, plan.grid
    edge, edge_turned = edges
    edge_plain, edge_mirror = swapped_edges
    me = lax.axis_index(AXES)
    mu, part = me // per_mu, me % per_mu
    partner = part >= per_mu // 2
    shared = (part == 0) & (mu >= tile // 2)
    head = jnp.where(shared, edge_plain, edge) + jnp.where(me == 0, edge_turned, edge_mirror)
    total = own + jnp.concatenate(received, axis=0).astype(F32)
    at_top = lax.broadcasted_iota(jnp.int32, total.shape, 1) == 0
    total = jnp.where(at_top & ~partner, head[:, None, :], total)
    extra = jnp.concatenate(
        [(edge_plain + edge_mirror)[:, None, :], jnp.zeros((devices, 7, rows), F32)], axis=1
    )
    return jnp.concatenate([total, extra], axis=1) * (0.5 / (grid * grid))


def local(charges, target, stencil, near_matrix, green, block_dest, block_tile, near_offset):
    devices = lax.axis_size(AXES)
    blocks, block_size, cell_count = stencil.shape
    pair_count = near_offset.shape[1]
    capacity = 2 * blocks // devices
    slots = devices * capacity
    plan = Plan(green.shape[0], math.isqrt(cell_count), devices)
    me = lax.axis_index(AXES)
    destination = block_dest[:, 0]
    one_hot = (destination[:, None] == jnp.arange(devices, dtype=jnp.int32)[None, :]).astype(
        jnp.int32
    )
    earlier = jnp.cumsum(one_hot, axis=0) - one_hot
    slot_index = destination * capacity + jnp.sum(earlier * one_hot, axis=1)
    spread = jnp.asarray(plan.spread_table())
    forward_table = jnp.asarray(plan.forward_table())
    inverse_table = jnp.asarray(plan.inverse_table())
    cosine, sine = (jnp.asarray(t) for t in plan.column_twiddles())
    edge_forward, edge_inverse = (jnp.asarray(t) for t in plan.edge_tables())
    both, row_cos, row_sin = (jnp.asarray(t) for t in plan.row_tables())
    origin = (me == 0).astype(jnp.int32).reshape(1)
    early, late, *edges = leaving_green(plan, green)
    spectrum_shape = jax.ShapeDtypeStruct((devices, plan.width, plan.rows), BF16)
    work_shape = (plan.tile // plan.group, plan.tile_cols, plan.group * plan.rows)

    def exchange(values):
        return lax.all_to_all(values, AXES, split_axis=0, concat_axis=0, tiled=True)

    def project(values, marked):
        tile_values = jnp.einsum("bp,bpt->bt", values, stencil, preferred_element_type=F32)
        if marked:
            named = jnp.broadcast_to((block_tile + 1).astype(F32)[:, None], (blocks, 128))
            tile_values = jnp.concatenate([tile_values, named], axis=1)
        outgoing = jnp.zeros((slots, tile_values.shape[1]), F32).at[slot_index].set(tile_values)
        return outgoing.reshape(devices, capacity, -1)

    def to_columns(arrived, marks):
        return kernel(
            forward_rows,
            plan,
            spectrum_shape,
            [pltpu.VMEM(work_shape, F32)],
            [],
            [arrived, marks, spread, forward_table, cosine, sine, edge_forward],
        )

    def along_columns(spectrum, weights):
        return kernel(
            columns,
            plan,
            spectrum_shape,
            [pltpu.VMEM((devices, 2 * (plan.half + 8), plan.rows), F32)],
            [origin],
            [spectrum, weights, both, row_cos, row_sin],
        )

    def to_rows(spectrum, marks):
        picked = kernel(
            inverse_rows,
            plan,
            jax.ShapeDtypeStruct((slots, cell_count), BF16),
            [pltpu.VMEM(work_shape, BF16)],
            [],
            [spectrum, marks, spread, inverse_table, cosine, sine, edge_inverse],
        )
        return picked.reshape(devices, capacity, cell_count)

    def interpolate(returned):
        own_tiles = returned.reshape(slots, cell_count)[slot_index]
        return jnp.einsum("bpt,bt->bp", stencil, own_tiles, preferred_element_type=F32)

    couple = near_matrix.reshape(blocks, pair_count, block_size, block_size)
    positions = jnp.arange(blocks, dtype=jnp.int32)[:, None] + REACH + near_offset
    charge_blocks = charges.reshape(blocks, block_size)
    extended = extended_2(charge_blocks, ((AXES, 0),), REACH)
    sources = extended[positions]

    early, late, edges = lax.optimization_barrier((early, late, edges))
    early = swap_mirrored(plan, early)
    outgoing, early, late = lax.optimization_barrier((project(charge_blocks, True), early, late))
    late = swap_mirrored(plan, late)
    swapped_edges = swap_edges(plan, *edges)
    arrived = exchange(outgoing).reshape(slots, -1)
    own = staying_green(plan, green)
    arrived, own = lax.optimization_barrier((arrived, own))
    marks = arrived[:, cell_count:]
    spectrum = to_columns(arrived[:, :cell_count], marks)
    spectrum, late, swapped_edges = lax.optimization_barrier((spectrum, late, swapped_edges))
    weights = symmetric_green(plan, own, (early, late), edges, swapped_edges)
    spectrum, couple, sources = lax.optimization_barrier((exchange(spectrum), couple, sources))
    picked = to_rows(exchange(along_columns(spectrum, weights)), marks)
    far = interpolate(exchange(picked))
    near = jnp.einsum("bkps,bks->bp", couple, sources, preferred_element_type=F32)
    potentials = far + near
    residual = (potentials - target.reshape(blocks, block_size)).astype(BF16)

    arrived = exchange(project(residual, False)).reshape(slots, -1)
    spectrum = exchange(to_columns(arrived, marks))
    spectrum = exchange(along_columns(spectrum, weights))
    terms = jnp.einsum("bkps,bp->bks", couple, residual, preferred_element_type=F32)
    extended = jnp.zeros((blocks + 2 * REACH, block_size), F32)
    extended = extended.at[positions.reshape(-1)].add(terms.reshape(-1, block_size))
    rims = jnp.concatenate([extended[:REACH], extended[blocks + REACH :]], axis=0)
    neighbour = extended_2(rims, ((AXES, 0),), REACH)
    own_part = extended[REACH : blocks + REACH]
    own_part = own_part.at[:REACH].add(neighbour[:REACH])
    own_part = own_part.at[blocks - REACH :].add(neighbour[3 * REACH :])
    gradient = interpolate(exchange(to_rows(spectrum, marks))) + own_part
    return (potentials.reshape(-1), gradient.reshape(-1))


def solution(mesh):
    rows = P(AXES)
    return jax.shard_map(
        local,
        mesh=mesh,
        in_specs=(rows, rows, rows, rows, P(None, AXES), rows, rows, rows),
        out_specs=(rows, rows),
        check_vma=False,
    )
```

```python
import functools
import math

import jax
import jax.numpy as jnp
import numpy as np
from jax import lax
from jax.experimental import pallas as pl
from jax.experimental.pallas import tpu as pltpu
from jax.sharding import PartitionSpec as P

REACH = 8
AXES = ("panel", "slab")
BF16 = jnp.bfloat16
F32 = jnp.float32
WIDE = 56 * 1024 * 1024
NARROW = 24 * 1024 * 1024
STEP = 16


def extended_2(cells, sides, width):
    for axis, dim in sides:
        count = lax.axis_size(axis)
        ends = count - 1
        head = lax.slice_in_dim(cells, 0, width, axis=dim)
        tail = lax.slice_in_dim(cells, cells.shape[dim] - width, cells.shape[dim], axis=dim)
        cells = jnp.concatenate(
            [
                lax.ppermute(tail, axis, [(i, (i + 1) % count) for i in range(ends)]),
                cells,
                lax.ppermute(head, axis, [((i + 1) % count, i) for i in range(ends)]),
            ],
            axis=dim,
        )
    return cells


def split(table):
    high = table.astype(jnp.bfloat16)
    return np.stack([high, (table - high.astype(np.float64)).astype(jnp.bfloat16)])


class Plan:
    def __init__(self, grid, tile, devices):
        self.grid, self.tile, self.devices = grid, tile, devices
        self.tile_cols = grid // tile
        self.rows = grid // devices
        self.width = grid // devices
        self.half = self.width // 2
        self.per_mu = devices // tile
        self.kappas = self.tile_cols // 2
        self.group = max(1, min(tile, 2 * 128 // self.rows))

    def factors(self):
        outer = 1 << ((self.devices.bit_length() - 1) // 2)
        return outer, self.devices // outer

    def low_part(self, index):
        outer, inner = self.factors()
        return index // inner + outer * (index % inner)

    def place_of(self, low):
        outer, inner = self.factors()
        return (low % outer) * inner + low // outer

    def place(self, position, mu):
        part, j = divmod(position, self.width)
        device = self.per_mu * mu + part
        if j < self.half:
            return device, j, 1.0
        return self.devices - 1 - device, j - self.half, -1.0

    def kappa(self):
        out = []
        for position in range(self.kappas):
            part, j = divmod(position, self.width)
            if j >= self.half:
                j = self.half + (self.half - (j - self.half)) % self.half
            out.append(self.width * part + j)
        return np.array(out)

    def forward_table(self):
        angle = 2 * np.pi * np.outer(self.kappa(), np.arange(self.tile_cols)) / self.tile_cols
        sine = -np.sin(angle)
        sine[0] = (-1.0) ** np.arange(self.tile_cols)
        return split(np.concatenate([np.cos(angle), sine]))

    def inverse_table(self):
        angle = 2 * np.pi * np.outer(np.arange(self.tile_cols), self.kappa()) / self.tile_cols
        cosine, sine = 2 * np.cos(angle), -2 * np.sin(angle)
        cosine[:, 0] = 1.0
        sine[:, 0] = (-1.0) ** np.arange(self.tile_cols)
        return split(np.concatenate([cosine, sine], axis=1))

    def column_twiddles(self):
        angle = 2 * np.pi * self.kappa() / self.grid
        full = np.broadcast_to(angle[:, None], (self.kappas, self.rows))
        return np.stack([np.cos(full), np.sin(full)]).astype(np.float32)

    def edge_tables(self):
        n, m = self.tile, self.tile // 2
        cells = np.arange(n)
        forward, inverse = np.zeros((2 * n, 2 * n)), np.zeros((2 * n, 2 * n))
        forward[0, :n], forward[n, :n] = 1.0, (-1.0) ** cells
        inverse[:n, 0], inverse[:n, n] = 1.0, (-1.0) ** cells
        for mu in range(1, m):
            angle = 2 * np.pi * cells * mu / n
            forward[mu, :n], forward[n + mu, :n] = np.cos(angle), -np.sin(angle)
            inverse[:n, mu], inverse[:n, n + mu] = 2 * np.cos(angle), -2 * np.sin(angle)
        for nu in range(m):
            angle = 2 * np.pi * cells * (1 + 2 * nu) / (2 * n)
            forward[m + nu, n:], forward[n + m + nu, n:] = np.cos(angle), -np.sin(angle)
            inverse[n:, m + nu], inverse[n:, n + m + nu] = 2 * np.cos(angle), -2 * np.sin(angle)
        return forward.astype(np.float32), inverse.astype(np.float32)

    def row_tables(self):
        n = self.rows
        angle = 2 * np.pi * (np.outer(np.arange(n), np.arange(n)) % n) / n
        both = split(np.concatenate([np.cos(angle), np.sin(angle)], axis=1))
        low = [self.low_part(index) for index in range(self.devices)]
        angle = 2 * np.pi * np.outer(low, np.arange(n)) / self.grid
        return both.reshape(2 * n, 2 * n), np.stack([np.cos(angle), np.sin(angle)]).astype(np.float32)

    def mirror_tables(self):
        pick = np.zeros((self.half + STEP, self.width))
        pick[self.half, 0] = 1.0
        for i in range(self.half):
            pick[i, self.width - i if i else self.half] = 1.0
        n = self.rows
        first, rest = np.zeros((n, n)), np.zeros((n, n))
        for i in range(n):
            first[(n - i) % n, i] = 1.0
            rest[n - 1 - i, i] = 1.0
        return pick.T.astype(jnp.bfloat16), np.stack([first, rest]).astype(jnp.bfloat16)


def transform(points, sign):
    count = len(points)
    if count == 1:
        return points
    even, odd = transform(points[0::2], sign), transform(points[1::2], sign)
    low, high = [], []
    for k in range(count // 2):
        (er, ei), (re, im) = even[k], odd[k]
        if 4 * k == count:
            re, im = (-im, re) if sign > 0 else (im, -re)
        elif 8 * k == count or 8 * k == 3 * count:
            root = math.sqrt(0.5)
            if 8 * k == count:
                re, im = (re - sign * im) * root, (im + sign * re) * root
            else:
                re, im = (-re - sign * im) * root, (sign * re - im) * root
        elif k:
            c, s = math.cos(2 * math.pi * k / count), sign * math.sin(2 * math.pi * k / count)
            re, im = re * c - im * s, im * c + re * s
        low.append((er + re, ei + im))
        high.append((er - re, ei - im))
    return low + high


def dot(a, b):
    return jnp.dot(a, b, preferred_element_type=F32)


def slot_tiles(marks, plan):
    number = marks.astype(jnp.int32) - 1
    shift = plan.tile_cols.bit_length() - 1
    return number & (plan.tile_cols - 1), number >> shift


def slot_mask(tile_row, plan):
    mine = tile_row[:, : plan.rows]
    lane = lax.broadcasted_iota(jnp.int32, mine.shape, 1) // plan.tile
    mask = (mine == lane).astype(F32)
    return jnp.concatenate([mask] * plan.group, axis=1) > 0.5


class Copies:
    def __init__(self, semaphores):
        self.semaphores, self.started = semaphores, []

    def start(self, source, target):
        copy = pltpu.make_async_copy(source, target, self.semaphores.at[len(self.started)])
        copy.start()
        self.started.append(copy)
        return copy

    def wait(self):
        for copy in self.started:
            copy.wait()


def cell_lanes(plan):
    cells, span = plan.tile * plan.tile, plan.group * plan.rows
    cell = lax.broadcasted_iota(jnp.int32, (cells, span), 0)
    lane = lax.broadcasted_iota(jnp.int32, (cells, span), 1)
    differs = (cell & (plan.tile - 1)) - lane // plan.rows
    return jnp.where(cell // plan.tile == (lane & (plan.tile - 1)), differs, -plan.tile)


def spread_lanes(plan, lanes, chunk):
    return jnp.where(lanes == chunk * plan.group, 1.0, 0.0).astype(BF16)


def powers(cosine, sine, count):
    out = [None, (cosine, sine)]
    for k in range(2, count):
        (c, s), (d, t) = out[k // 2], out[k - k // 2]
        out.append((c * d - s * t, s * d + c * t))
    return out


def forward_rows(plan, values_in, marked_in, table_in, twiddle_in, edge_in, out, values, marked, table, twiddle, edge, work, lines, ins, outs):
    tile, rows, group, half = plan.tile, plan.rows, plan.group, plan.half
    slots, cells = values.shape[0], tile * tile
    loads = Copies(ins)
    load_marks = loads.start(marked_in.at[:, cells:], marked)
    load_table = loads.start(table_in, table)
    load_values = loads.start(values_in.at[:, :cells], values)
    load_twiddle = loads.start(twiddle_in, twiddle)
    load_edge = loads.start(edge_in, edge)
    lanes = cell_lanes(plan)
    load_marks.wait()
    marks = marked[...]
    _, tile_row = slot_tiles(marks, plan)
    mask = slot_mask(tile_row, plan)
    tile_col, _ = slot_tiles(marks.T[0:1, :], plan)
    place = lax.broadcasted_iota(jnp.int32, (plan.tile_cols, slots), 0)
    chosen = (place == tile_col).astype(F32).astype(BF16)
    load_table.wait()
    weights = dot(table[0], chosen).astype(BF16)
    weights_low = dot(table[1], chosen).astype(BF16)
    load_values.wait()
    exact = values[...]
    high = exact.astype(BF16)
    low = (exact - high.astype(F32)).astype(BF16)
    for chunk in range(tile // group):
        spread = spread_lanes(plan, lanes, chunk)
        high_part = jnp.where(mask, dot(high, spread), 0.0).astype(BF16)
        low_part = jnp.where(mask, dot(low, spread), 0.0).astype(BF16)
        work[chunk] = (
            dot(weights, high_part) + dot(weights, low_part) + dot(weights_low, high_part)
        )
    load_twiddle.wait()
    load_edge.wait()

    def piece(cell, start, size):
        at = (cell % group) * rows
        return work[cell // group, start : start + size, at : at + rows]

    ends = [piece(cell, 0, 8)[0:1] for cell in range(tile)]
    ends += [piece(cell, plan.kappas, 8)[0:1] for cell in range(tile)]
    shared = jnp.dot(
        edge[...],
        jnp.concatenate(ends, axis=0),
        precision=lax.Precision.HIGHEST,
        preferred_element_type=F32,
    )
    first = lax.broadcasted_iota(jnp.int32, (STEP, rows), 0) == 0
    stores = Copies(outs)
    for start in range(0, plan.kappas, STEP):
        at = slice(start, start + STEP)
        turns = powers(twiddle[0, at], twiddle[1, at], tile)
        points = []
        for cell in range(tile):
            re, im = piece(cell, start, STEP), piece(cell, plan.kappas + start, STEP)
            if cell:
                c, s = turns[cell]
                re, im = re * c + im * s, im * c - re * s
            points.append((re, im))
        for mu, (re, im) in enumerate(transform(points, -1)):
            if start == 0:
                re = jnp.where(first, shared[mu : mu + 1], re)
                im = jnp.where(first, shared[tile + mu : tile + mu + 1], im)
            device, row, sign = plan.place(start, mu)
            lines[device, row : row + STEP] = re.astype(BF16)
            lines[device, half + row : half + row + STEP] = (im * sign).astype(BF16)
            if row + STEP == half:
                stores.start(lines.at[device], out.at[device])
    stores.wait()


def inverse_rows(plan, spectrum_in, marked_in, table_in, twiddle_in, edge_in, out, spectrum, marked, table, twiddle, edge, work, picked, ins, outs):
    tile, rows, group, half = plan.tile, plan.rows, plan.group, plan.half
    slots, cells = marked.shape[0], tile * tile
    loads = Copies(ins)
    load_marks = loads.start(marked_in.at[:, cells:], marked)
    load_edge = loads.start(edge_in, edge)
    load_rows = []
    for row in range(0, half, STEP):
        both_parts = []
        for at in (row, half + row):
            here = pl.ds(at, STEP)
            both_parts.append(loads.start(spectrum_in.at[:, here, :], spectrum.at[:, here, :]))
        load_rows.append(both_parts)
    load_twiddle = loads.start(twiddle_in, twiddle)
    load_table = loads.start(table_in, table)
    lanes = cell_lanes(plan)
    load_marks.wait()
    tile_col, tile_row = slot_tiles(marked[...], plan)
    mask = slot_mask(tile_row, plan)
    place = lax.broadcasted_iota(jnp.int32, (slots, plan.tile_cols), 1)
    chosen = (place == tile_col[:, 0:1]).astype(F32).astype(BF16)
    load_edge.wait()
    load_twiddle.wait()
    first = lax.broadcasted_iota(jnp.int32, (STEP, rows), 0) == 0
    for row in range(0, half, STEP):
        for copy in load_rows[row // STEP]:
            copy.wait()
        if row == 0:
            ends = [spectrum[plan.per_mu * mu, 0:STEP].astype(F32)[0:1] for mu in range(tile)]
            ends += [
                spectrum[plan.per_mu * mu, half : half + STEP].astype(F32)[0:1] for mu in range(tile)
            ]
            shared = jnp.dot(
                edge[...],
                jnp.concatenate(ends, axis=0),
                precision=lax.Precision.HIGHEST,
                preferred_element_type=F32,
            )
        for start in range(0, plan.kappas, STEP):
            if plan.place(start, 0)[1] != row:
                continue
            points = []
            for mu in range(tile):
                device, _, sign = plan.place(start, mu)
                re = spectrum[device, row : row + STEP].astype(F32)
                im = spectrum[device, half + row : half + row + STEP].astype(F32) * sign
                points.append((re, im))
            at = slice(start, start + STEP)
            second = slice(plan.kappas + start, plan.kappas + start + STEP)
            turns = powers(twiddle[0, at], twiddle[1, at], tile)
            for cell, (re, im) in enumerate(transform(points, 1)):
                if cell:
                    c, s = turns[cell]
                    re, im = re * c - im * s, im * c + re * s
                if start == 0:
                    re = jnp.where(first, shared[cell : cell + 1], re)
                    im = jnp.where(first, shared[tile + cell : tile + cell + 1], im)
                here = (cell % group) * rows
                work[cell // group, at, here : here + rows] = re.astype(BF16)
                work[cell // group, second, here : here + rows] = im.astype(BF16)
    load_table.wait()
    weights = dot(chosen, table[0]).astype(BF16)
    weights_low = dot(chosen, table[1]).astype(BF16)
    total = jnp.zeros(picked.shape, F32)
    for chunk in range(tile // group):
        field = dot(weights, work[chunk]) + dot(weights_low, work[chunk])
        field = jnp.where(mask, field, 0.0).astype(BF16)
        total = total + lax.dot_general(
            field,
            spread_lanes(plan, lanes, chunk),
            (((1,), (1,)), ((), ())),
            preferred_element_type=F32,
        )
    picked[...] = total.astype(BF16)
    stores = Copies(outs)
    stores.start(picked, out)
    stores.wait()


def turn_by(point, cosine, sine):
    re, im = point
    return re * cosine - im * sine, im * cosine + re * sine


def columns(plan, origin, spectrum_in, green_in, both_in, twiddle_in, out, spectrum, green, both, twiddle, result, work, rows16, ins, outs):
    loads, stores = Copies(ins), Copies(outs)
    arriving = start_columns(plan, loads, spectrum_in, spectrum, both_in, both, twiddle_in, twiddle)
    load_green = loads.start(green_in, green)
    every_column(
        plan, origin, arriving, spectrum, green, both, twiddle, load_green.wait, stores, out,
        result, work, rows16,
    )
    stores.wait()


def start_columns(plan, loads, spectrum_in, spectrum, both_in, both, twiddle_in, twiddle):
    arriving = []
    for start in range(0, plan.half, STEP):
        for at in (start, plan.half + start):
            here = pl.ds(at, STEP)
            arriving.append(loads.start(spectrum_in.at[:, here, :], spectrum.at[:, here, :]))
        if start == 0:
            arriving.append(loads.start(twiddle_in, twiddle))
            arriving.append(loads.start(both_in, both))
    return arriving


def every_column(plan, origin, arriving, spectrum, green, both, twiddle, need_green, stores, out, result, work, rows16):
    devices, rows, half = plan.devices, plan.rows, plan.half
    outer, inner = plan.factors()
    holds_edge = origin[0] == 1
    tall = 2 * half + STEP
    groups = [(start, half + start, STEP) for start in range(0, half, STEP)]
    groups.insert(1, (2 * half, 2 * half + 8, 8))
    top = (lax.broadcasted_iota(jnp.int32, (STEP, rows), 0) == 0) & holds_edge

    def constant(cell, low, sign):
        angle = 2 * math.pi * cell * low / devices
        return math.cos(angle), sign * math.sin(angle)

    def source(s, start):
        if start == 2 * half:
            shared = spectrum[s, half : half + STEP].astype(F32)
            return jnp.where(top, shared, 0.0)[0:8], jnp.zeros((8, rows), F32)
        re = spectrum[s, start : start + STEP].astype(F32)
        im = spectrum[s, half + start : half + start + STEP].astype(F32)
        return re, (jnp.where(top, 0.0, im) if start == 0 else im)

    arriving = list(arriving)
    for first, second, size in groups:
        at_re, at_im = slice(first, first + size), slice(second, second + size)
        if size == STEP:
            for copy in arriving[: 4 if first == 0 else 2]:
                copy.wait()
            arriving = arriving[4 if first == 0 else 2 :]
        for b in range(inner):
            points = [source(a * inner + b, first) for a in range(outer)]
            for low, point in enumerate(transform(points, -1)):
                if low and b:
                    point = turn_by(point, *constant(b, low, -1))
                work[low * inner + b, at_re], work[low * inner + b, at_im] = point
        for low in range(outer):
            base = low * inner
            points = [(work[base + b, at_re], work[base + b, at_im]) for b in range(inner)]
            for high, point in enumerate(transform(points, -1)):
                c, s = (twiddle[part, base + high : base + high + 1] for part in (0, 1))
                re, im = turn_by(point, c, -s)
                if size == 8:
                    both_parts = jnp.concatenate([re, im], axis=0)
                    rows16[base + high, 2 * half : tall] = both_parts.astype(BF16)
                else:
                    rows16[base + high, at_re] = re.astype(BF16)
                    rows16[base + high, at_im] = im.astype(BF16)
    need_green()
    batch = 4
    spans = [(0, half, 2 * half), (2 * half, 2 * half + 8, tall)]

    def product(values):
        flat = values.reshape(batch * tall, rows)
        twice = jnp.concatenate([flat, flat], axis=1)
        return dot(twice, both[...]).reshape(batch, tall, 2 * rows)

    def middle(i, carry):
        at = pl.ds(i * batch, batch)
        u = product(rows16[at])
        g = green[at]
        parts = []
        for (a, b, c), here in zip(spans, (g[:, :half], g[:, half:])):
            parts.append((u[:, a:b, :rows] + u[:, b:c, rows:]) * here)
            parts.append((u[:, b:c, :rows] - u[:, a:b, rows:]) * here)
        u = product(jnp.concatenate(parts, axis=1).astype(BF16))
        turn_c, turn_s = twiddle[0, at][:, None, :], twiddle[1, at][:, None, :]
        for a, b, c in spans:
            re = u[:, a:b, :rows] - u[:, b:c, rows:]
            im = u[:, b:c, :rows] + u[:, a:b, rows:]
            work[at, a:b], work[at, b:c] = turn_by((re, im), turn_c, turn_s)
        return carry

    lax.fori_loop(0, devices // batch, middle, 0)

    for first, second, size in [groups[1], groups[0], *groups[2:]]:
        at_re, at_im = slice(first, first + size), slice(second, second + size)
        for low in range(outer):
            base = low * inner
            points = [(work[base + high, at_re], work[base + high, at_im]) for high in range(inner)]
            for b, point in enumerate(transform(points, 1)):
                if low and b:
                    point = turn_by(point, *constant(b, low, 1))
                work[base + b, at_re], work[base + b, at_im] = point
        for b in range(inner):
            points = [
                (work[low * inner + b, at_re], work[low * inner + b, at_im])
                for low in range(outer)
            ]
            for a, (re, im) in enumerate(transform(points, 1)):
                s = a * inner + b
                if size == 8:
                    work[s, at_re] = re
                    continue
                if first == 0:
                    im = jnp.where(top, work[s, 2 * half : 2 * half + STEP], im)
                result[s, at_re] = re.astype(BF16)
                result[s, at_im] = im.astype(BF16)
        if size == STEP:
            for at in (first, second):
                here = pl.ds(at, STEP)
                stores.start(result.at[:, here, :], out.at[:, here, :])


def first_columns(plan, origin, follows, spectrum_in, own_in, early_in, late_in, head_in, extra_in, both_in, twiddle_in, out, weights_out, spectrum, green, both, twiddle, result, work, rows16, own, early, late, head, extra, ins, outs):
    half, rows, ahead = plan.half, plan.rows, early.shape[0]
    loads, stores = Copies(ins), Copies(outs)
    arriving = start_columns(plan, loads, spectrum_in, spectrum, both_in, both, twiddle_in, twiddle)
    parts = ((own_in, own), (early_in, early), (late_in, late), (head_in, head), (extra_in, extra))
    parts = [loads.start(source, target) for source, target in parts]

    def need_green():
        for copy in parts:
            copy.wait()
        scale = 0.5 / (plan.grid * plan.grid)
        replaced = lax.broadcasted_iota(jnp.int32, (half, rows), 0) == 0
        replaced = replaced & (follows[0] == 0)
        top = lax.broadcasted_iota(jnp.int32, (8, rows), 0) == 0
        for s in range(plan.devices):
            received = early[s] if s < ahead else late[s - ahead]
            total = own[s] + received.astype(F32)
            total = jnp.where(replaced, jnp.broadcast_to(head[s : s + 1], total.shape), total)
            green[s, 0:half] = total * scale
            second = jnp.broadcast_to(extra[s : s + 1], top.shape)
            green[s, half : half + 8] = jnp.where(top, second, 0.0) * scale
        stores.start(green, weights_out)

    every_column(
        plan, origin, arriving, spectrum, green, both, twiddle, need_green, stores, out,
        result, work, rows16,
    )
    stores.wait()


def mirrored_green(plan, green, pick, turn, early, late, edge, edge_turned, picked):
    devices, rows, half = plan.devices, plan.rows, plan.half
    picked[...] = dot(green[...].astype(BF16), pick[...])
    for m in range(devices):
        block = picked[pl.ds(m, rows, stride=devices), :].T
        turned = dot(block.astype(BF16), turn[0 if m == 0 else 1])
        here, there = plan.place_of(m), plan.place_of((devices - m) % devices)
        if there < early.shape[0]:
            early[there] = turned[0:half].astype(BF16)
        else:
            late[there - early.shape[0]] = turned[0:half].astype(BF16)
        edge[here : here + 1] = block[half : half + 1]
        edge_turned[there : there + 1] = turned[half : half + 1]


def own_green(plan, follows, green, own):
    devices, rows, half = plan.devices, plan.rows, plan.half
    partner = follows[0] == 1
    first = lax.broadcasted_iota(jnp.int32, (half, rows), 0) == 0
    for m in range(devices):
        turned = green[pl.ds(m, rows, stride=devices), :].T
        swap = jnp.broadcast_to(turned[half : half + 1], (half, rows))
        own[plan.place_of(m)] = jnp.where(first & partner, swap, turned[0:half])


def slot_choice(owners, capacity, slots):
    blocks = owners.shape[1]
    across = jnp.broadcast_to(owners[...].astype(F32), (blocks, blocks))
    first = lax.broadcasted_iota(jnp.int32, across.shape, 0)
    second = lax.broadcasted_iota(jnp.int32, across.shape, 1)
    earlier = jnp.where((across.T == across) & (first < second), 1.0, 0.0)
    slot = across[0:1] * capacity + jnp.sum(earlier, axis=0, keepdims=True)
    place = lax.broadcasted_iota(jnp.int32, (slots, blocks), 0)
    return jnp.where(place == slot.astype(jnp.int32), 1.0, 0.0)


def own_lanes(block_size):
    row = lax.broadcasted_iota(jnp.int32, (STEP, STEP * block_size), 0)
    lane = lax.broadcasted_iota(jnp.int32, (STEP, STEP * block_size), 1)
    return row == lane // block_size


def block_rows(stencil, group):
    _, block_size, cells = stencil.shape
    return stencil[group * STEP : (group + 1) * STEP].reshape(STEP * block_size, cells)


def start_blocks(loads, source, target):
    copies = []
    for group in range(source.shape[0] // STEP):
        here = pl.ds(group * STEP, STEP)
        copies.append(loads.start(source.at[here], target.at[here]))
    return copies


def project(values, stencil, chosen, need):
    mine = own_lanes(stencil.shape[1])
    tiles = []
    for group in range(values.shape[0]):
        spread = jnp.where(mine, jnp.broadcast_to(values[group : group + 1], mine.shape), 0.0)
        need(group)
        tiles.append(dot(spread.astype(BF16), block_rows(stencil, group)))
    tiles = jnp.concatenate(tiles, axis=0)
    high = tiles.astype(BF16)
    low = (tiles - high.astype(F32)).astype(BF16)
    return dot(chosen, high) + dot(chosen, low)


def interpolate(returned, stencil, chosen, need):
    mine = own_lanes(stencil.shape[1])
    own = lax.dot_general(
        chosen, returned[...], (((0,), (0,)), ((), ())), preferred_element_type=F32
    ).astype(BF16)
    far = []
    for group in range(stencil.shape[0] // STEP):
        need(group)
        every = lax.dot_general(
            own[group * STEP : (group + 1) * STEP],
            block_rows(stencil, group),
            (((1,), (1,)), ((), ())),
            preferred_element_type=F32,
        )
        far.append(jnp.sum(jnp.where(mine, every, 0.0), axis=0, keepdims=True))
    return jnp.concatenate(far, axis=0)


def first_tiles(capacity, owners_in, tiles_in, values_in, stencil_in, out, owners, tiles, values, stencil, tosend, ins, outs):
    slots, cells = out.shape[0], stencil.shape[2]
    loads, stores = Copies(ins), Copies(outs)
    small = [
        loads.start(owners_in, owners),
        loads.start(tiles_in, tiles),
        loads.start(values_in, values),
    ]
    blocks = start_blocks(loads, stencil_in, stencil)
    for copy in small:
        copy.wait()
    chosen = slot_choice(owners, capacity, slots)
    marks = jnp.sum(chosen * (tiles[...] + 1).astype(F32), axis=1, keepdims=True)
    tosend[:, cells:] = jnp.broadcast_to(marks, (slots, out.shape[1] - cells))
    tosend[:, :cells] = project(
        values[...].astype(F32), stencil, chosen.astype(BF16), lambda group: blocks[group].wait()
    )
    stores.start(tosend, out)
    stores.wait()


def middle_blocks(capacity, owners_in, returned_in, near_in, target_in, stencil_in, potentials, residual, out, owners, returned, near, target, stencil, tosend, ins, outs):
    loads, stores = Copies(ins), Copies(outs)
    first = [loads.start(owners_in, owners), loads.start(returned_in, returned)]
    blocks = start_blocks(loads, stencil_in, stencil)
    later = [loads.start(near_in, near), loads.start(target_in, target)]
    for copy in first:
        copy.wait()
    chosen = slot_choice(owners, capacity, out.shape[0]).astype(BF16)
    far = interpolate(returned, stencil, chosen, lambda group: blocks[group].wait())
    for copy in later:
        copy.wait()
    total = far + near[...]
    potentials[...] = total
    rounded = (total - target[...]).astype(BF16)
    residual[...] = rounded
    tosend[...] = project(rounded.astype(F32), stencil, chosen, lambda group: None)
    stores.start(tosend, out)
    stores.wait()


def last_blocks(capacity, owners_in, returned_in, near_in, stencil_in, gradient, owners, returned, near, stencil, ins):
    loads = Copies(ins)
    first = [loads.start(owners_in, owners), loads.start(returned_in, returned)]
    blocks = start_blocks(loads, stencil_in, stencil)
    last = loads.start(near_in, near)
    for copy in first:
        copy.wait()
    chosen = slot_choice(owners, capacity, returned.shape[0]).astype(BF16)
    far = interpolate(returned, stencil, chosen, lambda group: blocks[group].wait())
    last.wait()
    gradient[...] = far + near[...]


def kernel(body, plan, out_shape, scratch, scalars, operands):
    in_specs = [pl.BlockSpec(memory_space=pltpu.SMEM)] * len(scalars)
    in_specs += [pl.BlockSpec(memory_space=pltpu.VMEM)] * len(operands)
    return pl.pallas_call(
        functools.partial(body, plan),
        out_shape=out_shape,
        in_specs=in_specs,
        out_specs=jax.tree.map(lambda _: pl.BlockSpec(memory_space=pltpu.VMEM), out_shape),
        scratch_shapes=scratch,
        compiler_params=pltpu.CompilerParams(vmem_limit_bytes=WIDE),
    )(*scalars, *operands)


def streamed(
    body, plan, out_shape, out_spaces, scratch, copies, scalars, operands, grant=WIDE
):
    in_specs = [pl.BlockSpec(memory_space=pltpu.SMEM)] * len(scalars)
    in_specs += [pl.BlockSpec(memory_space=pl.ANY)] * len(operands)
    semaphores = [pltpu.SemaphoreType.DMA((count,)) for count in copies]
    return pl.pallas_call(
        functools.partial(body, plan),
        out_shape=out_shape,
        in_specs=in_specs,
        out_specs=jax.tree.map(lambda space: pl.BlockSpec(memory_space=space), out_spaces),
        scratch_shapes=[*scratch, *semaphores],
        compiler_params=pltpu.CompilerParams(vmem_limit_bytes=grant),
    )(*scalars, *operands)


def held(*arrays):
    return [pltpu.VMEM(array.shape, array.dtype) for array in arrays]


def leaving_green(plan, green):
    devices, half, rows = plan.devices, plan.half, plan.rows
    pick, turn = plan.mirror_tables()
    ahead = devices // 2
    early = jax.ShapeDtypeStruct((ahead, half, rows), BF16)
    late = jax.ShapeDtypeStruct((devices - ahead, half, rows), BF16)
    line = jax.ShapeDtypeStruct((devices, rows), F32)
    return kernel(
        mirrored_green,
        plan,
        (early, late, line, line),
        [pltpu.VMEM((plan.grid, half + STEP), F32)],
        [],
        [green, jnp.asarray(pick), jnp.asarray(turn)],
    )


def staying_green(plan, green):
    devices, half, rows, per_mu = plan.devices, plan.half, plan.rows, plan.per_mu
    partner = lax.axis_index(AXES) % per_mu >= per_mu // 2
    return kernel(
        own_green,
        plan,
        jax.ShapeDtypeStruct((devices, half, rows), F32),
        [],
        [partner.astype(jnp.int32).reshape(1)],
        [green],
    )


def swap_mirrored(plan, part):
    return lax.ppermute(part, AXES, [(i, plan.devices - 1 - i) for i in range(plan.devices)])


def swap_edges(plan, edge, edge_turned):
    devices, per_mu, tile = plan.devices, plan.per_mu, plan.tile
    upper = range(tile // 2, tile)
    plain = [(devices // 2, 0)]
    plain += [(per_mu * (m - tile // 2) + per_mu // 2, per_mu * m) for m in upper]
    mirror = [(devices // 2, 0)]
    mirror += [(per_mu * (tile - 1 - m + tile // 2) + per_mu // 2, per_mu * m) for m in upper]
    for i in range(1, devices):
        low = i % per_mu
        if low < per_mu // 2 and (low or i // per_mu < tile // 2):
            mirror.append((devices - i, i))
    return lax.ppermute(edge, AXES, plain), lax.ppermute(edge_turned, AXES, mirror)


def edge_lines(plan, edges, swapped_edges):
    edge, edge_turned = edges
    edge_plain, edge_mirror = swapped_edges
    me = lax.axis_index(AXES)
    mu, part = me // plan.per_mu, me % plan.per_mu
    shared = (part == 0) & (mu >= plan.tile // 2)
    head = jnp.where(shared, edge_plain, edge) + jnp.where(me == 0, edge_turned, edge_mirror)
    return head, edge_plain + edge_mirror


def local(charges, target, stencil, near_matrix, green, block_dest, block_tile, near_offset):
    devices = lax.axis_size(AXES)
    blocks, block_size, cell_count = stencil.shape
    pair_count = near_offset.shape[1]
    capacity = 2 * blocks // devices
    slots = devices * capacity
    plan = Plan(green.shape[0], math.isqrt(cell_count), devices)
    me = lax.axis_index(AXES)
    owners = block_dest.reshape(1, blocks)
    groups = (blocks // STEP, STEP * block_size)
    forward_table = jnp.asarray(plan.forward_table())
    inverse_table = jnp.asarray(plan.inverse_table())
    twiddle = jnp.asarray(plan.column_twiddles())
    edge_forward, edge_inverse = (jnp.asarray(t) for t in plan.edge_tables())
    both, row_twiddle = (jnp.asarray(t) for t in plan.row_tables())
    origin = (me == 0).astype(jnp.int32).reshape(1)
    partner = (me % plan.per_mu >= plan.per_mu // 2).astype(jnp.int32).reshape(1)
    early, late, *edges = leaving_green(plan, green)
    spectrum_shape = jax.ShapeDtypeStruct((devices, plan.width, plan.rows), BF16)
    tall_shape = (devices, 2 * plan.half + STEP, plan.rows)
    half_steps = plan.half // STEP
    green_shape = jax.ShapeDtypeStruct((devices, plan.half + 8, plan.rows), F32)
    column_work = [
        pltpu.VMEM(spectrum_shape.shape, BF16),
        pltpu.VMEM(tall_shape, F32),
        pltpu.VMEM(tall_shape, BF16),
    ]
    work_shape = (plan.tile // plan.group, plan.tile_cols, plan.group * plan.rows)

    def exchange(values):
        return lax.all_to_all(values, AXES, split_axis=0, concat_axis=0, tiled=True)

    def to_columns(arrived, marked, grant):
        return streamed(
            forward_rows,
            plan,
            spectrum_shape,
            pl.ANY,
            [
                pltpu.VMEM((slots, cell_count), F32),
                pltpu.VMEM((slots, 128), F32),
                *held(forward_table, twiddle, edge_forward),
                pltpu.VMEM(work_shape, F32),
                pltpu.VMEM(spectrum_shape.shape, BF16),
            ],
            (5, devices),
            [],
            [arrived, marked, forward_table, twiddle, edge_forward],
            grant,
        )

    def along_columns(spectrum, weights):
        return streamed(
            columns,
            plan,
            spectrum_shape,
            pl.ANY,
            [*held(spectrum, weights, both, row_twiddle), *column_work],
            (2 * half_steps + 3, 2 * half_steps),
            [origin],
            [spectrum, weights, both, row_twiddle],
            NARROW,
        )

    def to_rows(spectrum, marked):
        picked = streamed(
            inverse_rows,
            plan,
            jax.ShapeDtypeStruct((slots, cell_count), BF16),
            pl.ANY,
            [
                pltpu.VMEM(spectrum_shape.shape, BF16),
                pltpu.VMEM((slots, 128), F32),
                *held(inverse_table, twiddle, edge_inverse),
                pltpu.VMEM(work_shape, BF16),
                pltpu.VMEM((slots, cell_count), BF16),
            ],
            (2 * half_steps + 4, 1),
            [],
            [spectrum, marked, inverse_table, twiddle, edge_inverse],
            NARROW,
        )
        return exchange(picked.reshape(devices, capacity, cell_count)).reshape(slots, cell_count)

    couple = near_matrix.reshape(blocks, pair_count, block_size, block_size)
    positions = jnp.arange(blocks, dtype=jnp.int32)[:, None] + REACH + near_offset
    charge_blocks = charges.reshape(blocks, block_size)
    extended = extended_2(charge_blocks, ((AXES, 0),), REACH)
    sources = extended[positions]

    tiles = block_tile.reshape(1, blocks)
    values = charges.reshape(groups)
    outgoing_shape = jax.ShapeDtypeStruct((slots, cell_count + 128), F32)
    outgoing = streamed(
        first_tiles,
        capacity,
        outgoing_shape,
        pl.ANY,
        held(owners, tiles, values, stencil, outgoing_shape),
        (3 + groups[0], 1),
        [],
        [owners, tiles, values, stencil],
    )
    swapped_edges = swap_edges(plan, *edges)
    arrived = exchange(outgoing.reshape(devices, capacity, -1)).reshape(slots, -1)
    early = swap_mirrored(plan, early)
    arrived, late, edges, couple = lax.optimization_barrier((arrived, late, edges, couple))
    late = swap_mirrored(plan, late)
    marked = arrived
    spectrum = to_columns(arrived, marked, WIDE)
    spectrum, early = lax.optimization_barrier((spectrum, early))
    lines = edge_lines(plan, edges, swapped_edges)
    own = staying_green(plan, green)
    spectrum, couple, sources, own = lax.optimization_barrier(
        (exchange(spectrum), couple, sources, own)
    )
    green_parts = [own, early, late, *lines]
    spectrum, weights = streamed(
        first_columns,
        plan,
        (spectrum_shape, green_shape),
        (pl.ANY, pl.ANY),
        [
            *held(spectrum, green_shape, both, row_twiddle),
            *column_work,
            *held(*green_parts),
        ],
        (2 * half_steps + 2 + len(green_parts), 2 * half_steps + 1),
        [origin, partner],
        [spectrum, *green_parts, both, row_twiddle],
    )
    returned = to_rows(exchange(spectrum), marked)
    near = jnp.einsum("bkps,bks->bp", couple, sources, preferred_element_type=F32)
    near, target = near.reshape(groups), target.reshape(groups)
    outgoing_shape = jax.ShapeDtypeStruct((slots, cell_count), F32)
    potentials, residual, outgoing = streamed(
        middle_blocks,
        capacity,
        (
            jax.ShapeDtypeStruct(groups, F32),
            jax.ShapeDtypeStruct(groups, BF16),
            outgoing_shape,
        ),
        (pltpu.VMEM, pltpu.VMEM, pl.ANY),
        held(owners, returned, near, target, stencil, outgoing_shape),
        (4 + groups[0], 1),
        [],
        [owners, returned, near, target, stencil],
    )

    arrived = exchange(outgoing.reshape(devices, capacity, -1)).reshape(slots, -1)
    residual = residual.reshape(blocks, block_size)
    terms = jnp.einsum("bkps,bp->bks", couple, residual, preferred_element_type=F32)
    spectrum = exchange(to_columns(arrived, marked, NARROW))
    spectrum, terms = lax.optimization_barrier((spectrum, terms))
    spectrum = exchange(along_columns(spectrum, weights))
    extended = jnp.zeros((blocks + 2 * REACH, block_size), F32)
    extended = extended.at[positions.reshape(-1)].add(terms.reshape(-1, block_size))
    rims = jnp.concatenate([extended[:REACH], extended[blocks + REACH :]], axis=0)
    neighbour = extended_2(rims, ((AXES, 0),), REACH)
    own_part = extended[REACH : blocks + REACH]
    own_part = own_part.at[:REACH].add(neighbour[:REACH])
    own_part = own_part.at[blocks - REACH :].add(neighbour[3 * REACH :])
    returned, near = to_rows(spectrum, marked), own_part.reshape(groups)
    gradient = streamed(
        last_blocks,
        capacity,
        jax.ShapeDtypeStruct(groups, F32),
        pltpu.VMEM,
        held(owners, returned, near, stencil),
        (3 + groups[0],),
        [],
        [owners, returned, near, stencil],
    )
    return (potentials.reshape(-1), gradient.reshape(-1))


def solution(mesh):
    rows = P(AXES)
    return jax.shard_map(
        local,
        mesh=mesh,
        in_specs=(rows, rows, rows, rows, P(None, AXES), rows, rows, rows),
        out_specs=(rows, rows),
        check_vma=False,
    )
```

```python
import functools
import math

import jax
import jax.numpy as jnp
import numpy as np
from jax import lax
from jax.experimental import pallas as pl
from jax.experimental.pallas import tpu as pltpu
from jax.sharding import PartitionSpec as P

REACH = 8
AXES = ("panel", "slab")
BF16 = jnp.bfloat16
F32 = jnp.float32
WIDE = 56 * 1024 * 1024
NARROW = 24 * 1024 * 1024
STEP = 16
LANES = 128


def extended_2(cells, sides, width):
    for axis, dim in sides:
        count = lax.axis_size(axis)
        ends = count - 1
        head = lax.slice_in_dim(cells, 0, width, axis=dim)
        tail = lax.slice_in_dim(cells, cells.shape[dim] - width, cells.shape[dim], axis=dim)
        cells = jnp.concatenate(
            [
                lax.ppermute(tail, axis, [(i, (i + 1) % count) for i in range(ends)]),
                cells,
                lax.ppermute(head, axis, [((i + 1) % count, i) for i in range(ends)]),
            ],
            axis=dim,
        )
    return cells


def split(table):
    high = table.astype(jnp.bfloat16)
    return np.stack([high, (table - high.astype(np.float64)).astype(jnp.bfloat16)])


class Plan:
    def __init__(self, grid, tile, devices):
        self.grid, self.tile, self.devices = grid, tile, devices
        self.tile_cols = grid // tile
        self.rows = grid // devices
        self.width = grid // devices
        self.half = self.width // 2
        self.per_mu = devices // tile
        self.kappas = self.tile_cols // 2
        self.group = max(1, min(tile, 2 * 128 // self.rows))

    def factors(self):
        outer = 1 << ((self.devices.bit_length() - 1) // 2)
        return outer, self.devices // outer

    def low_part(self, index):
        outer, inner = self.factors()
        return index // inner + outer * (index % inner)

    def place_of(self, low):
        outer, inner = self.factors()
        return (low % outer) * inner + low // outer

    def place(self, position, mu):
        part, j = divmod(position, self.width)
        device = self.per_mu * mu + part
        if j < self.half:
            return device, j, 1.0
        return self.devices - 1 - device, j - self.half, -1.0

    def kappa(self):
        out = []
        for position in range(self.kappas):
            part, j = divmod(position, self.width)
            if j >= self.half:
                j = self.half + (self.half - (j - self.half)) % self.half
            out.append(self.width * part + j)
        return np.array(out)

    def forward_table(self):
        angle = 2 * np.pi * np.outer(self.kappa(), np.arange(self.tile_cols)) / self.tile_cols
        sine = -np.sin(angle)
        sine[0] = (-1.0) ** np.arange(self.tile_cols)
        return split(np.concatenate([np.cos(angle), sine]))

    def inverse_table(self):
        angle = 2 * np.pi * np.outer(np.arange(self.tile_cols), self.kappa()) / self.tile_cols
        cosine, sine = 2 * np.cos(angle), -2 * np.sin(angle)
        cosine[:, 0] = 1.0
        sine[:, 0] = (-1.0) ** np.arange(self.tile_cols)
        return split(np.concatenate([cosine, sine], axis=1))

    def column_twiddles(self):
        angle = 2 * np.pi * self.kappa() / self.grid
        full = np.broadcast_to(angle[:, None], (self.kappas, self.rows))
        return np.stack([np.cos(full), np.sin(full)]).astype(np.float32)

    def edge_tables(self):
        n, m = self.tile, self.tile // 2
        cells = np.arange(n)
        forward, inverse = np.zeros((2 * n, 2 * n)), np.zeros((2 * n, 2 * n))
        forward[0, :n], forward[n, :n] = 1.0, (-1.0) ** cells
        inverse[:n, 0], inverse[:n, n] = 1.0, (-1.0) ** cells
        for mu in range(1, m):
            angle = 2 * np.pi * cells * mu / n
            forward[mu, :n], forward[n + mu, :n] = np.cos(angle), -np.sin(angle)
            inverse[:n, mu], inverse[:n, n + mu] = 2 * np.cos(angle), -2 * np.sin(angle)
        for nu in range(m):
            angle = 2 * np.pi * cells * (1 + 2 * nu) / (2 * n)
            forward[m + nu, n:], forward[n + m + nu, n:] = np.cos(angle), -np.sin(angle)
            inverse[n:, m + nu], inverse[n:, n + m + nu] = 2 * np.cos(angle), -2 * np.sin(angle)
        return forward.astype(np.float32), inverse.astype(np.float32)

    def row_tables(self):
        n = self.rows
        angle = 2 * np.pi * (np.outer(np.arange(n), np.arange(n)) % n) / n
        both = split(np.concatenate([np.cos(angle), np.sin(angle)], axis=1))
        low = [self.low_part(index) for index in range(self.devices)]
        angle = 2 * np.pi * np.outer(low, np.arange(n)) / self.grid
        return both.reshape(2 * n, 2 * n), np.stack([np.cos(angle), np.sin(angle)]).astype(np.float32)

    def mirror_tables(self):
        pick = np.zeros((self.half + STEP, self.width))
        pick[self.half, 0] = 1.0
        for i in range(self.half):
            pick[i, self.width - i if i else self.half] = 1.0
        n = self.rows
        first, rest = np.zeros((n, n)), np.zeros((n, n))
        for i in range(n):
            first[(n - i) % n, i] = 1.0
            rest[n - 1 - i, i] = 1.0
        return pick.T.astype(jnp.bfloat16), np.stack([first, rest]).astype(jnp.bfloat16)


def transform(points, sign):
    count = len(points)
    if count == 1:
        return points
    even, odd = transform(points[0::2], sign), transform(points[1::2], sign)
    low, high = [], []
    for k in range(count // 2):
        (er, ei), (re, im) = even[k], odd[k]
        if 4 * k == count:
            re, im = (-im, re) if sign > 0 else (im, -re)
        elif 8 * k == count or 8 * k == 3 * count:
            root = math.sqrt(0.5)
            if 8 * k == count:
                re, im = (re - sign * im) * root, (im + sign * re) * root
            else:
                re, im = (-re - sign * im) * root, (sign * re - im) * root
        elif k:
            c, s = math.cos(2 * math.pi * k / count), sign * math.sin(2 * math.pi * k / count)
            re, im = re * c - im * s, im * c + re * s
        low.append((er + re, ei + im))
        high.append((er - re, ei - im))
    return low + high


def dot(a, b):
    return jnp.dot(a, b, preferred_element_type=F32)


def slot_tiles(marks, plan):
    number = marks.astype(jnp.int32) - 1
    shift = plan.tile_cols.bit_length() - 1
    return number & (plan.tile_cols - 1), number >> shift


def slot_mask(tile_row, plan):
    mine = tile_row[:, : plan.rows]
    lane = lax.broadcasted_iota(jnp.int32, mine.shape, 1) // plan.tile
    mask = (mine == lane).astype(F32)
    return jnp.concatenate([mask] * plan.group, axis=1) > 0.5


class Copies:
    def __init__(self, semaphores):
        self.semaphores, self.started = semaphores, []

    def start(self, source, target):
        copy = pltpu.make_async_copy(source, target, self.semaphores.at[len(self.started)])
        copy.start()
        self.started.append(copy)
        return copy

    def wait(self):
        for copy in self.started:
            copy.wait()


class Present:
    def wait(self):
        pass


def bring(loads, source, target):
    if target is None:
        return source, Present()
    return target, loads.start(source, target)


def cell_lanes(plan):
    cells, span = plan.tile * plan.tile, plan.group * plan.rows
    cell = lax.broadcasted_iota(jnp.int32, (cells, span), 0)
    lane = lax.broadcasted_iota(jnp.int32, (cells, span), 1)
    differs = (cell & (plan.tile - 1)) - lane // plan.rows
    return jnp.where(cell // plan.tile == (lane & (plan.tile - 1)), differs, -plan.tile)


def spread_lanes(plan, lanes, chunk):
    return jnp.where(lanes == chunk * plan.group, 1.0, 0.0).astype(BF16)


def powers(cosine, sine, count):
    out = [None, (cosine, sine)]
    for k in range(2, count):
        (c, s), (d, t) = out[k // 2], out[k - k // 2]
        out.append((c * d - s * t, s * d + c * t))
    return out


def resident_forward_rows(plan, values, marked, table, twiddle, edge, out, work, lines, outs):
    none = [None] * 5
    forward_rows(plan, values, marked, table, twiddle, edge, out, *none, work, lines, None, outs)


def forward_rows(plan, values_in, marked_in, table_in, twiddle_in, edge_in, out, values, marked, table, twiddle, edge, work, lines, ins, outs):
    tile, rows, group, half = plan.tile, plan.rows, plan.group, plan.half
    slots, cells = values_in.shape[0], tile * tile
    loads = Copies(ins)
    marked, load_marks = bring(loads, marked_in.at[:, cells:], marked)
    table, load_table = bring(loads, table_in, table)
    values, load_values = bring(loads, values_in.at[:, :cells], values)
    twiddle, load_twiddle = bring(loads, twiddle_in, twiddle)
    edge, load_edge = bring(loads, edge_in, edge)
    lanes = cell_lanes(plan)
    load_marks.wait()
    marks = marked[...]
    _, tile_row = slot_tiles(marks, plan)
    mask = slot_mask(tile_row, plan)
    tile_col, _ = slot_tiles(marks.T[0:1, :], plan)
    place = lax.broadcasted_iota(jnp.int32, (plan.tile_cols, slots), 0)
    chosen = (place == tile_col).astype(F32).astype(BF16)
    load_table.wait()
    weights = dot(table[0], chosen).astype(BF16)
    weights_low = dot(table[1], chosen).astype(BF16)
    load_values.wait()
    exact = values[...]
    high = exact.astype(BF16)
    low = (exact - high.astype(F32)).astype(BF16)
    for chunk in range(tile // group):
        spread = spread_lanes(plan, lanes, chunk)
        high_part = jnp.where(mask, dot(high, spread), 0.0).astype(BF16)
        low_part = jnp.where(mask, dot(low, spread), 0.0).astype(BF16)
        work[chunk] = (
            dot(weights, high_part) + dot(weights, low_part) + dot(weights_low, high_part)
        )
    load_twiddle.wait()
    load_edge.wait()

    def piece(cell, start, size):
        at = (cell % group) * rows
        return work[cell // group, start : start + size, at : at + rows]

    ends = [piece(cell, 0, 8)[0:1] for cell in range(tile)]
    ends += [piece(cell, plan.kappas, 8)[0:1] for cell in range(tile)]
    shared = jnp.dot(
        edge[...],
        jnp.concatenate(ends, axis=0),
        precision=lax.Precision.HIGHEST,
        preferred_element_type=F32,
    )
    first = lax.broadcasted_iota(jnp.int32, (STEP, rows), 0) == 0
    stores = Copies(outs)
    for start in range(0, plan.kappas, STEP):
        at = slice(start, start + STEP)
        turns = powers(twiddle[0, at], twiddle[1, at], tile)
        points = []
        for cell in range(tile):
            re, im = piece(cell, start, STEP), piece(cell, plan.kappas + start, STEP)
            if cell:
                c, s = turns[cell]
                re, im = re * c + im * s, im * c - re * s
            points.append((re, im))
        for mu, (re, im) in enumerate(transform(points, -1)):
            if start == 0:
                re = jnp.where(first, shared[mu : mu + 1], re)
                im = jnp.where(first, shared[tile + mu : tile + mu + 1], im)
            device, row, sign = plan.place(start, mu)
            lines[device, row : row + STEP] = re.astype(BF16)
            lines[device, half + row : half + row + STEP] = (im * sign).astype(BF16)
            if row + STEP == half:
                stores.start(lines.at[device], out.at[device])
    stores.wait()


def inverse_rows(plan, spectrum, marked, table, twiddle, edge, out, work, picked, outs):
    tile, rows, group, half = plan.tile, plan.rows, plan.group, plan.half
    slots, cells = marked.shape[0], tile * tile
    lanes = cell_lanes(plan)
    tile_col, tile_row = slot_tiles(marked[:, cells:], plan)
    mask = slot_mask(tile_row, plan)
    place = lax.broadcasted_iota(jnp.int32, (slots, plan.tile_cols), 1)
    chosen = (place == tile_col[:, 0:1]).astype(F32).astype(BF16)
    first = lax.broadcasted_iota(jnp.int32, (STEP, rows), 0) == 0
    for row in range(0, half, STEP):
        if row == 0:
            ends = [spectrum[plan.per_mu * mu, 0:STEP].astype(F32)[0:1] for mu in range(tile)]
            ends += [
                spectrum[plan.per_mu * mu, half : half + STEP].astype(F32)[0:1] for mu in range(tile)
            ]
            shared = jnp.dot(
                edge[...],
                jnp.concatenate(ends, axis=0),
                precision=lax.Precision.HIGHEST,
                preferred_element_type=F32,
            )
        for start in range(0, plan.kappas, STEP):
            if plan.place(start, 0)[1] != row:
                continue
            points = []
            for mu in range(tile):
                device, _, sign = plan.place(start, mu)
                re = spectrum[device, row : row + STEP].astype(F32)
                im = spectrum[device, half + row : half + row + STEP].astype(F32) * sign
                points.append((re, im))
            at = slice(start, start + STEP)
            second = slice(plan.kappas + start, plan.kappas + start + STEP)
            turns = powers(twiddle[0, at], twiddle[1, at], tile)
            for cell, (re, im) in enumerate(transform(points, 1)):
                if cell:
                    c, s = turns[cell]
                    re, im = re * c - im * s, im * c + re * s
                if start == 0:
                    re = jnp.where(first, shared[cell : cell + 1], re)
                    im = jnp.where(first, shared[tile + cell : tile + cell + 1], im)
                here = (cell % group) * rows
                work[cell // group, at, here : here + rows] = re.astype(BF16)
                work[cell // group, second, here : here + rows] = im.astype(BF16)
    weights = dot(chosen, table[0]).astype(BF16)
    weights_low = dot(chosen, table[1]).astype(BF16)
    total = jnp.zeros(picked.shape, F32)
    for chunk in range(tile // group):
        field = dot(weights, work[chunk]) + dot(weights_low, work[chunk])
        field = jnp.where(mask, field, 0.0).astype(BF16)
        total = total + lax.dot_general(
            field,
            spread_lanes(plan, lanes, chunk),
            (((1,), (1,)), ((), ())),
            preferred_element_type=F32,
        )
    picked[...] = total.astype(BF16)
    stores = Copies(outs)
    stores.start(picked, out)
    stores.wait()


def turn_by(point, cosine, sine):
    re, im = point
    return re * cosine - im * sine, im * cosine + re * sine


def columns(plan, origin, spectrum, green, both, twiddle, out, result, work, rows16, outs):
    stores = Copies(outs)
    every_column(
        plan, origin, [], spectrum, green, both, twiddle, lambda: None, stores, out,
        result, work, rows16,
    )
    stores.wait()


def start_columns(plan, loads, spectrum_in, spectrum, both_in, both, twiddle_in, twiddle):
    arriving = []
    for start in range(0, plan.half, STEP):
        for at in (start, plan.half + start):
            here = pl.ds(at, STEP)
            arriving.append(loads.start(spectrum_in.at[:, here, :], spectrum.at[:, here, :]))
        if start == 0:
            arriving.append(loads.start(twiddle_in, twiddle))
            arriving.append(loads.start(both_in, both))
    return arriving


def every_column(plan, origin, arriving, spectrum, green, both, twiddle, need_green, stores, out, result, work, rows16):
    devices, rows, half = plan.devices, plan.rows, plan.half
    outer, inner = plan.factors()
    holds_edge = origin[0] == 1
    tall = 2 * half + STEP
    groups = [(start, half + start, STEP) for start in range(0, half, STEP)]
    groups.insert(1, (2 * half, 2 * half + 8, 8))
    top = (lax.broadcasted_iota(jnp.int32, (STEP, rows), 0) == 0) & holds_edge

    def constant(cell, low, sign):
        angle = 2 * math.pi * cell * low / devices
        return math.cos(angle), sign * math.sin(angle)

    def source(s, start):
        if start == 2 * half:
            shared = spectrum[s, half : half + STEP].astype(F32)
            return jnp.where(top, shared, 0.0)[0:8], jnp.zeros((8, rows), F32)
        re = spectrum[s, start : start + STEP].astype(F32)
        im = spectrum[s, half + start : half + start + STEP].astype(F32)
        return re, (jnp.where(top, 0.0, im) if start == 0 else im)

    arriving = list(arriving)
    for first, second, size in groups:
        at_re, at_im = slice(first, first + size), slice(second, second + size)
        if size == STEP:
            for copy in arriving[: 4 if first == 0 else 2]:
                copy.wait()
            arriving = arriving[4 if first == 0 else 2 :]
        for b in range(inner):
            points = [source(a * inner + b, first) for a in range(outer)]
            for low, point in enumerate(transform(points, -1)):
                if low and b:
                    point = turn_by(point, *constant(b, low, -1))
                work[low * inner + b, at_re], work[low * inner + b, at_im] = point
        for low in range(outer):
            base = low * inner
            points = [(work[base + b, at_re], work[base + b, at_im]) for b in range(inner)]
            for high, point in enumerate(transform(points, -1)):
                c, s = (twiddle[part, base + high : base + high + 1] for part in (0, 1))
                re, im = turn_by(point, c, -s)
                if size == 8:
                    both_parts = jnp.concatenate([re, im], axis=0)
                    rows16[base + high, 2 * half : tall] = both_parts.astype(BF16)
                else:
                    rows16[base + high, at_re] = re.astype(BF16)
                    rows16[base + high, at_im] = im.astype(BF16)
    need_green()
    batch = 4
    spans = [(0, half, 2 * half), (2 * half, 2 * half + 8, tall)]

    def product(values):
        flat = values.reshape(batch * tall, rows)
        twice = jnp.concatenate([flat, flat], axis=1)
        return dot(twice, both[...]).reshape(batch, tall, 2 * rows)

    def middle(i, carry):
        at = pl.ds(i * batch, batch)
        u = product(rows16[at])
        g = green[at]
        parts = []
        for (a, b, c), here in zip(spans, (g[:, :half], g[:, half:])):
            parts.append((u[:, a:b, :rows] + u[:, b:c, rows:]) * here)
            parts.append((u[:, b:c, :rows] - u[:, a:b, rows:]) * here)
        u = product(jnp.concatenate(parts, axis=1).astype(BF16))
        turn_c, turn_s = twiddle[0, at][:, None, :], twiddle[1, at][:, None, :]
        for a, b, c in spans:
            re = u[:, a:b, :rows] - u[:, b:c, rows:]
            im = u[:, b:c, :rows] + u[:, a:b, rows:]
            work[at, a:b], work[at, b:c] = turn_by((re, im), turn_c, turn_s)
        return carry

    lax.fori_loop(0, devices // batch, middle, 0)

    for first, second, size in [groups[1], groups[0], *groups[2:]]:
        at_re, at_im = slice(first, first + size), slice(second, second + size)
        for low in range(outer):
            base = low * inner
            points = [(work[base + high, at_re], work[base + high, at_im]) for high in range(inner)]
            for b, point in enumerate(transform(points, 1)):
                if low and b:
                    point = turn_by(point, *constant(b, low, 1))
                work[base + b, at_re], work[base + b, at_im] = point
        for b in range(inner):
            points = [
                (work[low * inner + b, at_re], work[low * inner + b, at_im])
                for low in range(outer)
            ]
            for a, (re, im) in enumerate(transform(points, 1)):
                s = a * inner + b
                if size == 8:
                    work[s, at_re] = re
                    continue
                if first == 0:
                    im = jnp.where(top, work[s, 2 * half : 2 * half + STEP], im)
                result[s, at_re] = re.astype(BF16)
                result[s, at_im] = im.astype(BF16)
        if size == STEP:
            for at in (first, second):
                here = pl.ds(at, STEP)
                stores.start(result.at[:, here, :], out.at[:, here, :])


def first_columns(plan, origin, follows, spectrum_in, own_in, early_in, late_in, head_in, extra_in, both_in, twiddle_in, out, weights_out, spectrum, green, both, twiddle, result, work, rows16, own, early, late, head, extra, ins, outs):
    half, rows, ahead = plan.half, plan.rows, early.shape[0]
    loads, stores = Copies(ins), Copies(outs)
    arriving = start_columns(plan, loads, spectrum_in, spectrum, both_in, both, twiddle_in, twiddle)
    parts = ((own_in, own), (early_in, early), (late_in, late), (head_in, head), (extra_in, extra))
    parts = [loads.start(source, target) for source, target in parts]

    def need_green():
        for copy in parts:
            copy.wait()
        scale = 0.5 / (plan.grid * plan.grid)
        replaced = lax.broadcasted_iota(jnp.int32, (half, rows), 0) == 0
        replaced = replaced & (follows[0] == 0)
        top = lax.broadcasted_iota(jnp.int32, (8, rows), 0) == 0
        for s in range(plan.devices):
            received = early[s] if s < ahead else late[s - ahead]
            total = own[s] + received.astype(F32)
            total = jnp.where(replaced, jnp.broadcast_to(head[s : s + 1], total.shape), total)
            green[s, 0:half] = total * scale
            second = jnp.broadcast_to(extra[s : s + 1], top.shape)
            green[s, half : half + 8] = jnp.where(top, second, 0.0) * scale
        stores.start(green, weights_out)

    every_column(
        plan, origin, arriving, spectrum, green, both, twiddle, need_green, stores, out,
        result, work, rows16,
    )
    stores.wait()


def mirrored_green(plan, green, pick, turn, early, late, edge, edge_turned, picked):
    devices, rows, half = plan.devices, plan.rows, plan.half
    picked[...] = dot(green[...].astype(BF16), pick[...])
    for m in range(devices):
        block = picked[pl.ds(m, rows, stride=devices), :].T
        turned = dot(block.astype(BF16), turn[0 if m == 0 else 1])
        here, there = plan.place_of(m), plan.place_of((devices - m) % devices)
        if there < early.shape[0]:
            early[there] = turned[0:half].astype(BF16)
        else:
            late[there - early.shape[0]] = turned[0:half].astype(BF16)
        edge[here : here + 1] = block[half : half + 1]
        edge_turned[there : there + 1] = turned[half : half + 1]


def own_green(plan, follows, green, own):
    devices, rows, half = plan.devices, plan.rows, plan.half
    partner = follows[0] == 1
    first = lax.broadcasted_iota(jnp.int32, (half, rows), 0) == 0
    for m in range(devices):
        turned = green[pl.ds(m, rows, stride=devices), :].T
        swap = jnp.broadcast_to(turned[half : half + 1], (half, rows))
        own[plan.place_of(m)] = jnp.where(first & partner, swap, turned[0:half])


def slot_choice(owners, capacity, slots):
    blocks = owners.shape[1]
    across = jnp.broadcast_to(owners[...].astype(F32), (blocks, blocks))
    first = lax.broadcasted_iota(jnp.int32, across.shape, 0)
    second = lax.broadcasted_iota(jnp.int32, across.shape, 1)
    earlier = jnp.where((across.T == across) & (first < second), 1.0, 0.0)
    slot = across[0:1] * capacity + jnp.sum(earlier, axis=0, keepdims=True)
    place = lax.broadcasted_iota(jnp.int32, (slots, blocks), 0)
    return jnp.where(place == slot.astype(jnp.int32), 1.0, 0.0)


def own_lanes(block_size):
    row = lax.broadcasted_iota(jnp.int32, (STEP, STEP * block_size), 0)
    lane = lax.broadcasted_iota(jnp.int32, (STEP, STEP * block_size), 1)
    return row == lane // block_size


def block_rows(stencil, group):
    _, block_size, cells = stencil.shape
    return stencil[group * STEP : (group + 1) * STEP].reshape(STEP * block_size, cells)


def start_blocks(loads, source, target):
    copies = []
    for group in range(source.shape[0] // STEP):
        here = pl.ds(group * STEP, STEP)
        copies.append(loads.start(source.at[here], target.at[here]))
    return copies


def project(values, stencil, chosen, need):
    mine = own_lanes(stencil.shape[1])
    each = mine.shape[1] // LANES
    tiles = []
    for group in range(stencil.shape[0] // STEP):
        rows = [values[i : i + 1] for i in range(group * each, (group + 1) * each)]
        spread = jnp.concatenate([jnp.broadcast_to(row, (STEP, LANES)) for row in rows], axis=1)
        need(group)
        spread = jnp.where(mine, spread, 0.0).astype(BF16)
        tiles.append(dot(spread, block_rows(stencil, group)))
    tiles = jnp.concatenate(tiles, axis=0)
    high = tiles.astype(BF16)
    low = (tiles - high.astype(F32)).astype(BF16)
    return dot(chosen, high) + dot(chosen, low)


def interpolate(returned, stencil, chosen, need):
    mine = own_lanes(stencil.shape[1])
    own = lax.dot_general(
        chosen, returned[...], (((0,), (0,)), ((), ())), preferred_element_type=F32
    ).astype(BF16)
    far = []
    for group in range(stencil.shape[0] // STEP):
        need(group)
        every = lax.dot_general(
            own[group * STEP : (group + 1) * STEP],
            block_rows(stencil, group),
            (((1,), (1,)), ((), ())),
            preferred_element_type=F32,
        )
        sums = jnp.sum(jnp.where(mine, every, 0.0), axis=0, keepdims=True)
        far += [sums[:, i : i + LANES] for i in range(0, mine.shape[1], LANES)]
    return jnp.concatenate(far, axis=0)


def first_tiles(capacity, owners_in, tiles_in, values_in, stencil_in, out, owners, tiles, values, stencil, tosend, ins, outs):
    slots, cells = out.shape[0], stencil.shape[2]
    loads, stores = Copies(ins), Copies(outs)
    small = [
        loads.start(owners_in, owners),
        loads.start(tiles_in, tiles),
        loads.start(values_in, values),
    ]
    blocks = start_blocks(loads, stencil_in, stencil)
    for copy in small:
        copy.wait()
    chosen = slot_choice(owners, capacity, slots)
    marks = jnp.sum(chosen * (tiles[...] + 1).astype(F32), axis=1, keepdims=True)
    tosend[:, cells:] = jnp.broadcast_to(marks, (slots, out.shape[1] - cells))
    tosend[:, :cells] = project(
        values[...].astype(F32), stencil, chosen.astype(BF16), lambda group: blocks[group].wait()
    )
    stores.start(tosend, out)
    stores.wait()


def middle_blocks(capacity, owners_in, returned_in, near_in, target_in, stencil_in, potentials, residual, out, owners, returned, near, target, stencil, tosend, ins, outs):
    loads, stores = Copies(ins), Copies(outs)
    load_owners = loads.start(owners_in, owners)
    load_returned = loads.start(returned_in, returned)
    blocks = start_blocks(loads, stencil_in, stencil)
    later = [loads.start(near_in, near), loads.start(target_in, target)]
    load_owners.wait()
    chosen = slot_choice(owners, capacity, out.shape[0]).astype(BF16)
    load_returned.wait()
    far = interpolate(returned, stencil, chosen, lambda group: blocks[group].wait())
    for copy in later:
        copy.wait()
    total = far + near[...]
    potentials[...] = total
    rounded = (total - target[...]).astype(BF16)
    residual[...] = rounded
    tosend[...] = project(rounded.astype(F32), stencil, chosen, lambda group: None)
    stores.start(tosend, out)
    stores.wait()


def last_blocks(capacity, owners_in, returned_in, near_in, stencil_in, gradient, owners, returned, near, stencil, ins):
    loads = Copies(ins)
    load_owners = loads.start(owners_in, owners)
    load_returned = loads.start(returned_in, returned)
    blocks = start_blocks(loads, stencil_in, stencil)
    last = loads.start(near_in, near)
    load_owners.wait()
    chosen = slot_choice(owners, capacity, returned.shape[0]).astype(BF16)
    load_returned.wait()
    far = interpolate(returned, stencil, chosen, lambda group: blocks[group].wait())
    last.wait()
    gradient[...] = far + near[...]


def kernel(body, plan, out_shape, scratch, scalars, operands):
    in_specs = [pl.BlockSpec(memory_space=pltpu.SMEM)] * len(scalars)
    in_specs += [pl.BlockSpec(memory_space=pltpu.VMEM)] * len(operands)
    return pl.pallas_call(
        functools.partial(body, plan),
        out_shape=out_shape,
        in_specs=in_specs,
        out_specs=jax.tree.map(lambda _: pl.BlockSpec(memory_space=pltpu.VMEM), out_shape),
        scratch_shapes=scratch,
        compiler_params=pltpu.CompilerParams(vmem_limit_bytes=WIDE),
    )(*scalars, *operands)


def streamed(
    body, plan, out_shape, out_spaces, scratch, copies, scalars, operands, grant=WIDE
):
    space = pl.ANY if grant == WIDE else pltpu.VMEM
    in_specs = [pl.BlockSpec(memory_space=pltpu.SMEM)] * len(scalars)
    in_specs += [pl.BlockSpec(memory_space=space)] * len(operands)
    semaphores = [pltpu.SemaphoreType.DMA((count,)) for count in copies]
    return pl.pallas_call(
        functools.partial(body, plan),
        out_shape=out_shape,
        in_specs=in_specs,
        out_specs=jax.tree.map(lambda space: pl.BlockSpec(memory_space=space), out_spaces),
        scratch_shapes=[*scratch, *semaphores],
        compiler_params=pltpu.CompilerParams(vmem_limit_bytes=grant),
    )(*scalars, *operands)


def held(*arrays):
    return [pltpu.VMEM(array.shape, array.dtype) for array in arrays]


def leaving_green(plan, green):
    devices, half, rows = plan.devices, plan.half, plan.rows
    pick, turn = plan.mirror_tables()
    ahead = devices // 2
    early = jax.ShapeDtypeStruct((ahead, half, rows), BF16)
    late = jax.ShapeDtypeStruct((devices - ahead, half, rows), BF16)
    line = jax.ShapeDtypeStruct((devices, rows), F32)
    return kernel(
        mirrored_green,
        plan,
        (early, late, line, line),
        [pltpu.VMEM((plan.grid, half + STEP), F32)],
        [],
        [green, jnp.asarray(pick), jnp.asarray(turn)],
    )


def staying_green(plan, green):
    devices, half, rows, per_mu = plan.devices, plan.half, plan.rows, plan.per_mu
    partner = lax.axis_index(AXES) % per_mu >= per_mu // 2
    return kernel(
        own_green,
        plan,
        jax.ShapeDtypeStruct((devices, half, rows), F32),
        [],
        [partner.astype(jnp.int32).reshape(1)],
        [green],
    )


def swap_mirrored(plan, part):
    return lax.ppermute(part, AXES, [(i, plan.devices - 1 - i) for i in range(plan.devices)])


def swap_edges(plan, edge, edge_turned):
    devices, per_mu, tile = plan.devices, plan.per_mu, plan.tile
    upper = range(tile // 2, tile)
    plain = [(devices // 2, 0)]
    plain += [(per_mu * (m - tile // 2) + per_mu // 2, per_mu * m) for m in upper]
    mirror = [(devices // 2, 0)]
    mirror += [(per_mu * (tile - 1 - m + tile // 2) + per_mu // 2, per_mu * m) for m in upper]
    for i in range(1, devices):
        low = i % per_mu
        if low < per_mu // 2 and (low or i // per_mu < tile // 2):
            mirror.append((devices - i, i))
    return lax.ppermute(edge, AXES, plain), lax.ppermute(edge_turned, AXES, mirror)


def edge_lines(plan, edges, swapped_edges):
    edge, edge_turned = edges
    edge_plain, edge_mirror = swapped_edges
    me = lax.axis_index(AXES)
    mu, part = me // plan.per_mu, me % plan.per_mu
    shared = (part == 0) & (mu >= plan.tile // 2)
    head = jnp.where(shared, edge_plain, edge) + jnp.where(me == 0, edge_turned, edge_mirror)
    return head, edge_plain + edge_mirror


def local(charges, target, stencil, near_matrix, green, block_dest, block_tile, near_offset):
    devices = lax.axis_size(AXES)
    blocks, block_size, cell_count = stencil.shape
    pair_count = near_offset.shape[1]
    capacity = 2 * blocks // devices
    slots = devices * capacity
    plan = Plan(green.shape[0], math.isqrt(cell_count), devices)
    me = lax.axis_index(AXES)
    owners = block_dest.reshape(1, blocks)
    flat = (blocks * block_size // LANES, LANES)
    steps = blocks // STEP
    forward_table = jnp.asarray(plan.forward_table())
    inverse_table = jnp.asarray(plan.inverse_table())
    twiddle = jnp.asarray(plan.column_twiddles())
    edge_forward, edge_inverse = (jnp.asarray(t) for t in plan.edge_tables())
    both, row_twiddle = (jnp.asarray(t) for t in plan.row_tables())
    origin = (me == 0).astype(jnp.int32).reshape(1)
    partner = (me % plan.per_mu >= plan.per_mu // 2).astype(jnp.int32).reshape(1)
    early, late, *edges = leaving_green(plan, green)
    spectrum_shape = jax.ShapeDtypeStruct((devices, plan.width, plan.rows), BF16)
    tall_shape = (devices, 2 * plan.half + STEP, plan.rows)
    half_steps = plan.half // STEP
    green_shape = jax.ShapeDtypeStruct((devices, plan.half + 8, plan.rows), F32)
    column_work = [
        pltpu.VMEM(spectrum_shape.shape, BF16),
        pltpu.VMEM(tall_shape, F32),
        pltpu.VMEM(tall_shape, BF16),
    ]
    work_shape = (plan.tile // plan.group, plan.tile_cols, plan.group * plan.rows)

    def exchange(values):
        return lax.all_to_all(values, AXES, split_axis=0, concat_axis=0, tiled=True)

    def to_columns(arrived, marked, grant):
        operands = [arrived, marked, forward_table, twiddle, edge_forward]
        copied = [pltpu.VMEM((slots, cell_count), F32), pltpu.VMEM((slots, 128), F32)]
        copied += held(forward_table, twiddle, edge_forward)
        wide = grant == WIDE
        return streamed(
            forward_rows if wide else resident_forward_rows,
            plan,
            spectrum_shape,
            pl.ANY,
            [
                *(copied if wide else []),
                pltpu.VMEM(work_shape, F32),
                pltpu.VMEM(spectrum_shape.shape, BF16),
            ],
            (5, devices) if wide else (devices,),
            [],
            operands,
            grant,
        )

    def along_columns(spectrum, weights):
        return streamed(
            columns,
            plan,
            spectrum_shape,
            pl.ANY,
            column_work,
            (2 * half_steps,),
            [origin],
            [spectrum, weights, both, row_twiddle],
            NARROW,
        )

    def to_rows(spectrum, marked):
        picked = streamed(
            inverse_rows,
            plan,
            jax.ShapeDtypeStruct((slots, cell_count), BF16),
            pl.ANY,
            [pltpu.VMEM(work_shape, BF16), pltpu.VMEM((slots, cell_count), BF16)],
            (1,),
            [],
            [spectrum, marked, inverse_table, twiddle, edge_inverse],
            NARROW,
        )
        return exchange(picked.reshape(devices, capacity, cell_count)).reshape(slots, cell_count)

    couple = near_matrix.reshape(blocks, pair_count, block_size, block_size)
    positions = jnp.arange(blocks, dtype=jnp.int32)[:, None] + REACH + near_offset
    charge_blocks = charges.reshape(blocks, block_size)
    sources = extended_2(charge_blocks, ((AXES, 0),), REACH)[positions]

    tiles = block_tile.reshape(1, blocks)
    values = charges.reshape(flat)
    outgoing_shape = jax.ShapeDtypeStruct((slots, cell_count + 128), F32)
    outgoing = streamed(
        first_tiles,
        capacity,
        outgoing_shape,
        pl.ANY,
        held(owners, tiles, values, stencil, outgoing_shape),
        (3 + steps, 1),
        [],
        [owners, tiles, values, stencil],
    )
    swapped_edges = swap_edges(plan, *edges)
    arrived = exchange(outgoing.reshape(devices, capacity, -1)).reshape(slots, -1)
    early = swap_mirrored(plan, early)
    arrived, late, edges, couple = lax.optimization_barrier((arrived, late, edges, couple))
    late = swap_mirrored(plan, late)
    marked = arrived
    spectrum = to_columns(arrived, marked, WIDE)
    spectrum, early = lax.optimization_barrier((spectrum, early))
    lines = edge_lines(plan, edges, swapped_edges)
    own = staying_green(plan, green)
    spectrum, couple, sources, own = lax.optimization_barrier(
        (exchange(spectrum), couple, sources, own)
    )
    green_parts = [own, early, late, *lines]
    spectrum, weights = streamed(
        first_columns,
        plan,
        (spectrum_shape, green_shape),
        (pl.ANY, pl.ANY),
        [
            *held(spectrum, green_shape, both, row_twiddle),
            *column_work,
            *held(*green_parts),
        ],
        (2 * half_steps + 2 + len(green_parts), 2 * half_steps + 1),
        [origin, partner],
        [spectrum, *green_parts, both, row_twiddle],
    )
    returned = to_rows(exchange(spectrum), marked)
    near = jnp.einsum("bkps,bks->bp", couple, sources, preferred_element_type=F32)
    near, target = near.reshape(flat), target.reshape(flat)
    outgoing_shape = jax.ShapeDtypeStruct((slots, cell_count), F32)
    potentials, residual, outgoing = streamed(
        middle_blocks,
        capacity,
        (
            jax.ShapeDtypeStruct(flat, F32),
            jax.ShapeDtypeStruct(flat, BF16),
            outgoing_shape,
        ),
        (pltpu.VMEM, pltpu.VMEM, pl.ANY),
        held(owners, returned, near, target, stencil, outgoing_shape),
        (4 + steps, 1),
        [],
        [owners, returned, near, target, stencil],
    )

    arrived = exchange(outgoing.reshape(devices, capacity, -1)).reshape(slots, -1)
    residual = residual.reshape(blocks, block_size)
    terms = jnp.einsum("bkps,bp->bks", couple, residual, preferred_element_type=F32)
    spectrum = exchange(to_columns(arrived, marked, NARROW))
    spectrum, terms = lax.optimization_barrier((spectrum, terms))
    spectrum = exchange(along_columns(spectrum, weights))
    extended = jnp.zeros((blocks + 2 * REACH, block_size), F32)
    extended = extended.at[positions.reshape(-1)].add(terms.reshape(-1, block_size))
    rims = jnp.concatenate([extended[:REACH], extended[blocks + REACH :]], axis=0)
    neighbour = extended_2(rims, ((AXES, 0),), REACH)
    own_part = extended[REACH : blocks + REACH]
    own_part = own_part.at[:REACH].add(neighbour[:REACH])
    own_part = own_part.at[blocks - REACH :].add(neighbour[3 * REACH :])
    returned = to_rows(spectrum, marked)
    near = own_part.reshape(flat)
    gradient = streamed(
        last_blocks,
        capacity,
        jax.ShapeDtypeStruct(flat, F32),
        pltpu.VMEM,
        held(owners, returned, near, stencil),
        (3 + steps,),
        [],
        [owners, returned, near, stencil],
    )
    return (potentials.reshape(-1), gradient.reshape(-1))


def solution(mesh):
    rows = P(AXES)
    return jax.shard_map(
        local,
        mesh=mesh,
        in_specs=(rows, rows, rows, rows, P(None, AXES), rows, rows, rows),
        out_specs=(rows, rows),
        check_vma=False,
    )
```

```python
import functools
import math

import jax
import jax.numpy as jnp
import numpy as np
from jax import lax
from jax.experimental import pallas as pl
from jax.experimental.pallas import tpu as pltpu
from jax.sharding import PartitionSpec as P

REACH = 8
AXES = ("panel", "slab")
BF16 = jnp.bfloat16
F32 = jnp.float32
WIDE = 56 * 1024 * 1024
NARROW = 24 * 1024 * 1024
STEP = 16
LANES = 128


def extended_2(cells, sides, width):
    for axis, dim in sides:
        count = lax.axis_size(axis)
        ends = count - 1
        head = lax.slice_in_dim(cells, 0, width, axis=dim)
        tail = lax.slice_in_dim(cells, cells.shape[dim] - width, cells.shape[dim], axis=dim)
        cells = jnp.concatenate(
            [
                lax.ppermute(tail, axis, [(i, (i + 1) % count) for i in range(ends)]),
                cells,
                lax.ppermute(head, axis, [((i + 1) % count, i) for i in range(ends)]),
            ],
            axis=dim,
        )
    return cells


def split(table):
    high = table.astype(jnp.bfloat16)
    return np.stack([high, (table - high.astype(np.float64)).astype(jnp.bfloat16)])


class Plan:
    def __init__(self, grid, tile, devices):
        self.grid, self.tile, self.devices = grid, tile, devices
        self.tile_cols = grid // tile
        self.rows = grid // devices
        self.width = grid // devices
        self.half = self.width // 2
        self.per_mu = devices // tile
        self.kappas = self.tile_cols // 2
        self.group = max(1, min(tile, 2 * 128 // self.rows))

    def factors(self):
        outer = 1 << ((self.devices.bit_length() - 1) // 2)
        return outer, self.devices // outer

    def low_part(self, index):
        outer, inner = self.factors()
        return index // inner + outer * (index % inner)

    def place_of(self, low):
        outer, inner = self.factors()
        return (low % outer) * inner + low // outer

    def place(self, position, mu):
        part, j = divmod(position, self.width)
        device = self.per_mu * mu + part
        if j < self.half:
            return device, j, 1.0
        return self.devices - 1 - device, j - self.half, -1.0

    def kappa(self):
        out = []
        for position in range(self.kappas):
            part, j = divmod(position, self.width)
            if j >= self.half:
                j = self.half + (self.half - (j - self.half)) % self.half
            out.append(self.width * part + j)
        return np.array(out)

    def forward_table(self):
        angle = 2 * np.pi * np.outer(self.kappa(), np.arange(self.tile_cols)) / self.tile_cols
        sine = -np.sin(angle)
        sine[0] = (-1.0) ** np.arange(self.tile_cols)
        return split(np.concatenate([np.cos(angle), sine]))

    def inverse_table(self):
        angle = 2 * np.pi * np.outer(np.arange(self.tile_cols), self.kappa()) / self.tile_cols
        cosine, sine = 2 * np.cos(angle), -2 * np.sin(angle)
        cosine[:, 0] = 1.0
        sine[:, 0] = (-1.0) ** np.arange(self.tile_cols)
        return split(np.concatenate([cosine, sine], axis=1))

    def column_twiddles(self):
        angle = 2 * np.pi * self.kappa() / self.grid
        full = np.broadcast_to(angle[:, None], (self.kappas, self.rows))
        return np.stack([np.cos(full), np.sin(full)]).astype(np.float32)

    def edge_tables(self):
        n, m = self.tile, self.tile // 2
        cells = np.arange(n)
        forward, inverse = np.zeros((2 * n, 2 * n)), np.zeros((2 * n, 2 * n))
        forward[0, :n], forward[n, :n] = 1.0, (-1.0) ** cells
        inverse[:n, 0], inverse[:n, n] = 1.0, (-1.0) ** cells
        for mu in range(1, m):
            angle = 2 * np.pi * cells * mu / n
            forward[mu, :n], forward[n + mu, :n] = np.cos(angle), -np.sin(angle)
            inverse[:n, mu], inverse[:n, n + mu] = 2 * np.cos(angle), -2 * np.sin(angle)
        for nu in range(m):
            angle = 2 * np.pi * cells * (1 + 2 * nu) / (2 * n)
            forward[m + nu, n:], forward[n + m + nu, n:] = np.cos(angle), -np.sin(angle)
            inverse[n:, m + nu], inverse[n:, n + m + nu] = 2 * np.cos(angle), -2 * np.sin(angle)
        return forward.astype(np.float32), inverse.astype(np.float32)

    def row_tables(self):
        n = self.rows
        angle = 2 * np.pi * (np.outer(np.arange(n), np.arange(n)) % n) / n
        both = split(np.concatenate([np.cos(angle), np.sin(angle)], axis=1))
        low = [self.low_part(index) for index in range(self.devices)]
        angle = 2 * np.pi * np.outer(low, np.arange(n)) / self.grid
        return both.reshape(2 * n, 2 * n), np.stack([np.cos(angle), np.sin(angle)]).astype(np.float32)

    def mirror_tables(self):
        pick = np.zeros((self.half + STEP, self.width))
        pick[self.half, 0] = 1.0
        for i in range(self.half):
            pick[i, self.width - i if i else self.half] = 1.0
        n = self.rows
        first, rest = np.zeros((n, n)), np.zeros((n, n))
        for i in range(n):
            first[(n - i) % n, i] = 1.0
            rest[n - 1 - i, i] = 1.0
        return pick.T.astype(jnp.bfloat16), np.stack([first, rest]).astype(jnp.bfloat16)


def transform(points, sign):
    count = len(points)
    if count == 1:
        return points
    even, odd = transform(points[0::2], sign), transform(points[1::2], sign)
    low, high = [], []
    for k in range(count // 2):
        (er, ei), (re, im) = even[k], odd[k]
        if 4 * k == count:
            re, im = (-im, re) if sign > 0 else (im, -re)
        elif 8 * k == count or 8 * k == 3 * count:
            root = math.sqrt(0.5)
            if 8 * k == count:
                re, im = (re - sign * im) * root, (im + sign * re) * root
            else:
                re, im = (-re - sign * im) * root, (sign * re - im) * root
        elif k:
            c, s = math.cos(2 * math.pi * k / count), sign * math.sin(2 * math.pi * k / count)
            re, im = re * c - im * s, im * c + re * s
        low.append((er + re, ei + im))
        high.append((er - re, ei - im))
    return low + high


def dot(a, b):
    return jnp.dot(a, b, preferred_element_type=F32)


def slot_tiles(marks, plan):
    number = marks.astype(jnp.int32) - 1
    shift = plan.tile_cols.bit_length() - 1
    return number & (plan.tile_cols - 1), number >> shift


def slot_mask(tile_row, plan):
    mine = tile_row[:, : plan.rows]
    lane = lax.broadcasted_iota(jnp.int32, mine.shape, 1) // plan.tile
    mask = (mine == lane).astype(F32)
    return jnp.concatenate([mask] * plan.group, axis=1) > 0.5


class Copies:
    def __init__(self, semaphores):
        self.semaphores, self.started = semaphores, []

    def start(self, source, target):
        copy = pltpu.make_async_copy(source, target, self.semaphores.at[len(self.started)])
        copy.start()
        self.started.append(copy)
        return copy

    def wait(self):
        for copy in self.started:
            copy.wait()


class Present:
    def wait(self):
        pass


def bring(loads, source, target):
    if target is None:
        return source, Present()
    return target, loads.start(source, target)


def cell_lanes(plan):
    cells, span = plan.tile * plan.tile, plan.group * plan.rows
    cell = lax.broadcasted_iota(jnp.int32, (cells, span), 0)
    lane = lax.broadcasted_iota(jnp.int32, (cells, span), 1)
    differs = (cell & (plan.tile - 1)) - lane // plan.rows
    return jnp.where(cell // plan.tile == (lane & (plan.tile - 1)), differs, -plan.tile)


def spread_lanes(plan, lanes, chunk):
    return jnp.where(lanes == chunk * plan.group, 1.0, 0.0).astype(BF16)


def powers(cosine, sine, count):
    out = [None, (cosine, sine)]
    for k in range(2, count):
        (c, s), (d, t) = out[k // 2], out[k - k // 2]
        out.append((c * d - s * t, s * d + c * t))
    return out


def resident_forward_rows(plan, values, marked, table, twiddle, edge, out, work, lines, outs):
    none = [None] * 5
    forward_rows(plan, values, marked, table, twiddle, edge, out, *none, work, lines, None, outs)


def forward_rows(plan, values_in, marked_in, table_in, twiddle_in, edge_in, out, values, marked, table, twiddle, edge, work, lines, ins, outs):
    tile, rows, group, half = plan.tile, plan.rows, plan.group, plan.half
    slots, cells = values_in.shape[0], tile * tile
    loads = Copies(ins)
    marked, load_marks = bring(loads, marked_in.at[:, cells:], marked)
    table, load_table = bring(loads, table_in, table)
    values, load_values = bring(loads, values_in.at[:, :cells], values)
    twiddle, load_twiddle = bring(loads, twiddle_in, twiddle)
    edge, load_edge = bring(loads, edge_in, edge)
    lanes = cell_lanes(plan)
    load_marks.wait()
    marks = marked[...]
    _, tile_row = slot_tiles(marks, plan)
    mask = slot_mask(tile_row, plan)
    tile_col, _ = slot_tiles(marks.T[0:1, :], plan)
    place = lax.broadcasted_iota(jnp.int32, (plan.tile_cols, slots), 0)
    chosen = (place == tile_col).astype(F32).astype(BF16)
    load_table.wait()
    weights = dot(table[0], chosen).astype(BF16)
    weights_low = dot(table[1], chosen).astype(BF16)
    load_values.wait()
    exact = values[...]
    high = exact.astype(BF16)
    low = (exact - high.astype(F32)).astype(BF16)
    for chunk in range(tile // group):
        spread = spread_lanes(plan, lanes, chunk)
        high_part = jnp.where(mask, dot(high, spread), 0.0).astype(BF16)
        low_part = jnp.where(mask, dot(low, spread), 0.0).astype(BF16)
        work[chunk] = (
            dot(weights, high_part) + dot(weights, low_part) + dot(weights_low, high_part)
        )
    load_twiddle.wait()
    load_edge.wait()

    def piece(cell, start, size):
        at = (cell % group) * rows
        return work[cell // group, start : start + size, at : at + rows]

    ends = [piece(cell, 0, 8)[0:1] for cell in range(tile)]
    ends += [piece(cell, plan.kappas, 8)[0:1] for cell in range(tile)]
    shared = jnp.dot(
        edge[...],
        jnp.concatenate(ends, axis=0),
        precision=lax.Precision.HIGHEST,
        preferred_element_type=F32,
    )
    first = lax.broadcasted_iota(jnp.int32, (STEP, rows), 0) == 0
    stores = Copies(outs)
    for start in range(0, plan.kappas, STEP):
        at = slice(start, start + STEP)
        turns = powers(twiddle[0, at], twiddle[1, at], tile)
        points = []
        for cell in range(tile):
            re, im = piece(cell, start, STEP), piece(cell, plan.kappas + start, STEP)
            if cell:
                c, s = turns[cell]
                re, im = re * c + im * s, im * c - re * s
            points.append((re, im))
        for mu, (re, im) in enumerate(transform(points, -1)):
            if start == 0:
                re = jnp.where(first, shared[mu : mu + 1], re)
                im = jnp.where(first, shared[tile + mu : tile + mu + 1], im)
            device, row, sign = plan.place(start, mu)
            lines[device, row : row + STEP] = re.astype(BF16)
            lines[device, half + row : half + row + STEP] = (im * sign).astype(BF16)
            if row + STEP == half:
                stores.start(lines.at[device], out.at[device])
    stores.wait()


def inverse_rows(plan, spectrum, marked, table, twiddle, edge, out, work, picked, outs):
    tile, rows, group, half = plan.tile, plan.rows, plan.group, plan.half
    slots, cells = marked.shape[0], tile * tile
    lanes = cell_lanes(plan)
    tile_col, tile_row = slot_tiles(marked[:, cells:], plan)
    mask = slot_mask(tile_row, plan)
    place = lax.broadcasted_iota(jnp.int32, (slots, plan.tile_cols), 1)
    chosen = (place == tile_col[:, 0:1]).astype(F32).astype(BF16)
    first = lax.broadcasted_iota(jnp.int32, (STEP, rows), 0) == 0
    for row in range(0, half, STEP):
        if row == 0:
            ends = [spectrum[plan.per_mu * mu, 0:STEP].astype(F32)[0:1] for mu in range(tile)]
            ends += [
                spectrum[plan.per_mu * mu, half : half + STEP].astype(F32)[0:1] for mu in range(tile)
            ]
            shared = jnp.dot(
                edge[...],
                jnp.concatenate(ends, axis=0),
                precision=lax.Precision.HIGHEST,
                preferred_element_type=F32,
            )
        for start in range(0, plan.kappas, STEP):
            if plan.place(start, 0)[1] != row:
                continue
            points = []
            for mu in range(tile):
                device, _, sign = plan.place(start, mu)
                re = spectrum[device, row : row + STEP].astype(F32)
                im = spectrum[device, half + row : half + row + STEP].astype(F32) * sign
                points.append((re, im))
            at = slice(start, start + STEP)
            second = slice(plan.kappas + start, plan.kappas + start + STEP)
            turns = powers(twiddle[0, at], twiddle[1, at], tile)
            for cell, (re, im) in enumerate(transform(points, 1)):
                if cell:
                    c, s = turns[cell]
                    re, im = re * c - im * s, im * c + re * s
                if start == 0:
                    re = jnp.where(first, shared[cell : cell + 1], re)
                    im = jnp.where(first, shared[tile + cell : tile + cell + 1], im)
                here = (cell % group) * rows
                work[cell // group, at, here : here + rows] = re.astype(BF16)
                work[cell // group, second, here : here + rows] = im.astype(BF16)
    weights = dot(chosen, table[0]).astype(BF16)
    weights_low = dot(chosen, table[1]).astype(BF16)
    total = jnp.zeros(picked.shape, F32)
    for chunk in range(tile // group):
        field = dot(weights, work[chunk]) + dot(weights_low, work[chunk])
        field = jnp.where(mask, field, 0.0).astype(BF16)
        total = total + lax.dot_general(
            field,
            spread_lanes(plan, lanes, chunk),
            (((1,), (1,)), ((), ())),
            preferred_element_type=F32,
        )
    picked[...] = total.astype(BF16)
    stores = Copies(outs)
    stores.start(picked, out)
    stores.wait()


def turn_by(point, cosine, sine):
    re, im = point
    return re * cosine - im * sine, im * cosine + re * sine


def columns(plan, origin, spectrum, green, both, twiddle, out, result, work, rows16, outs):
    stores = Copies(outs)
    every_column(
        plan, origin, [], spectrum, green, both, twiddle, lambda: None, stores, out,
        result, work, rows16,
    )
    stores.wait()


def start_columns(plan, loads, spectrum_in, spectrum, both_in, both, twiddle_in, twiddle):
    arriving = []
    for start in range(0, plan.half, STEP):
        for at in (start, plan.half + start):
            here = pl.ds(at, STEP)
            arriving.append(loads.start(spectrum_in.at[:, here, :], spectrum.at[:, here, :]))
        if start == 0:
            arriving.append(loads.start(twiddle_in, twiddle))
            arriving.append(loads.start(both_in, both))
    return arriving


def every_column(plan, origin, arriving, spectrum, green, both, twiddle, need_green, stores, out, result, work, rows16):
    devices, rows, half = plan.devices, plan.rows, plan.half
    outer, inner = plan.factors()
    holds_edge = origin[0] == 1
    tall = 2 * half + STEP
    groups = [(start, half + start, STEP) for start in range(0, half, STEP)]
    groups.insert(1, (2 * half, 2 * half + 8, 8))
    top = (lax.broadcasted_iota(jnp.int32, (STEP, rows), 0) == 0) & holds_edge

    def constant(cell, low, sign):
        angle = 2 * math.pi * cell * low / devices
        return math.cos(angle), sign * math.sin(angle)

    def source(s, start):
        if start == 2 * half:
            shared = spectrum[s, half : half + STEP].astype(F32)
            return jnp.where(top, shared, 0.0)[0:8], jnp.zeros((8, rows), F32)
        re = spectrum[s, start : start + STEP].astype(F32)
        im = spectrum[s, half + start : half + start + STEP].astype(F32)
        return re, (jnp.where(top, 0.0, im) if start == 0 else im)

    arriving = list(arriving)
    for first, second, size in groups:
        at_re, at_im = slice(first, first + size), slice(second, second + size)
        if size == STEP:
            for copy in arriving[: 4 if first == 0 else 2]:
                copy.wait()
            arriving = arriving[4 if first == 0 else 2 :]
        for b in range(inner):
            points = [source(a * inner + b, first) for a in range(outer)]
            for low, point in enumerate(transform(points, -1)):
                if low and b:
                    point = turn_by(point, *constant(b, low, -1))
                work[low * inner + b, at_re], work[low * inner + b, at_im] = point
        for low in range(outer):
            base = low * inner
            points = [(work[base + b, at_re], work[base + b, at_im]) for b in range(inner)]
            for high, point in enumerate(transform(points, -1)):
                c, s = (twiddle[part, base + high : base + high + 1] for part in (0, 1))
                re, im = turn_by(point, c, -s)
                if size == 8:
                    both_parts = jnp.concatenate([re, im], axis=0)
                    rows16[base + high, 2 * half : tall] = both_parts.astype(BF16)
                else:
                    rows16[base + high, at_re] = re.astype(BF16)
                    rows16[base + high, at_im] = im.astype(BF16)
    need_green()
    batch = 4
    spans = [(0, half, 2 * half), (2 * half, 2 * half + 8, tall)]

    def product(values):
        flat = values.reshape(batch * tall, rows)
        twice = jnp.concatenate([flat, flat], axis=1)
        return dot(twice, both[...]).reshape(batch, tall, 2 * rows)

    def middle(i, carry):
        at = pl.ds(i * batch, batch)
        u = product(rows16[at])
        g = green[at]
        parts = []
        for (a, b, c), here in zip(spans, (g[:, :half], g[:, half:])):
            parts.append((u[:, a:b, :rows] + u[:, b:c, rows:]) * here)
            parts.append((u[:, b:c, :rows] - u[:, a:b, rows:]) * here)
        u = product(jnp.concatenate(parts, axis=1).astype(BF16))
        turn_c, turn_s = twiddle[0, at][:, None, :], twiddle[1, at][:, None, :]
        for a, b, c in spans:
            re = u[:, a:b, :rows] - u[:, b:c, rows:]
            im = u[:, b:c, :rows] + u[:, a:b, rows:]
            work[at, a:b], work[at, b:c] = turn_by((re, im), turn_c, turn_s)
        return carry

    lax.fori_loop(0, devices // batch, middle, 0, unroll=4)

    for first, second, size in [groups[1], groups[0], *groups[2:]]:
        at_re, at_im = slice(first, first + size), slice(second, second + size)
        for low in range(outer):
            base = low * inner
            points = [(work[base + high, at_re], work[base + high, at_im]) for high in range(inner)]
            for b, point in enumerate(transform(points, 1)):
                if low and b:
                    point = turn_by(point, *constant(b, low, 1))
                work[base + b, at_re], work[base + b, at_im] = point
        for b in range(inner):
            points = [
                (work[low * inner + b, at_re], work[low * inner + b, at_im])
                for low in range(outer)
            ]
            for a, (re, im) in enumerate(transform(points, 1)):
                s = a * inner + b
                if size == 8:
                    work[s, at_re] = re
                    continue
                if first == 0:
                    im = jnp.where(top, work[s, 2 * half : 2 * half + STEP], im)
                result[s, at_re] = re.astype(BF16)
                result[s, at_im] = im.astype(BF16)
        if size == STEP:
            for at in (first, second):
                here = pl.ds(at, STEP)
                stores.start(result.at[:, here, :], out.at[:, here, :])


def first_columns(plan, origin, follows, spectrum_in, own_in, early_in, late_in, head_in, extra_in, both_in, twiddle_in, out, weights_out, spectrum, green, both, twiddle, result, work, rows16, own, early, late, head, extra, ins, outs):
    half, rows, ahead = plan.half, plan.rows, early.shape[0]
    loads, stores = Copies(ins), Copies(outs)
    arriving = start_columns(plan, loads, spectrum_in, spectrum, both_in, both, twiddle_in, twiddle)
    parts = ((own_in, own), (early_in, early), (late_in, late), (head_in, head), (extra_in, extra))
    parts = [loads.start(source, target) for source, target in parts]

    def need_green():
        for copy in parts:
            copy.wait()
        scale = 0.5 / (plan.grid * plan.grid)
        replaced = lax.broadcasted_iota(jnp.int32, (half, rows), 0) == 0
        replaced = replaced & (follows[0] == 0)
        top = lax.broadcasted_iota(jnp.int32, (8, rows), 0) == 0
        for s in range(plan.devices):
            received = early[s] if s < ahead else late[s - ahead]
            total = own[s] + received.astype(F32)
            total = jnp.where(replaced, jnp.broadcast_to(head[s : s + 1], total.shape), total)
            green[s, 0:half] = total * scale
            second = jnp.broadcast_to(extra[s : s + 1], top.shape)
            green[s, half : half + 8] = jnp.where(top, second, 0.0) * scale
        stores.start(green, weights_out)

    every_column(
        plan, origin, arriving, spectrum, green, both, twiddle, need_green, stores, out,
        result, work, rows16,
    )
    stores.wait()


def mirrored_green(plan, green, pick, turn, early, late, edge, edge_turned, picked):
    devices, rows, half = plan.devices, plan.rows, plan.half
    picked[...] = dot(green[...].astype(BF16), pick[...])
    for m in range(devices):
        block = picked[pl.ds(m, rows, stride=devices), :].T
        turned = dot(block.astype(BF16), turn[0 if m == 0 else 1])
        here, there = plan.place_of(m), plan.place_of((devices - m) % devices)
        if there < early.shape[0]:
            early[there] = turned[0:half].astype(BF16)
        else:
            late[there - early.shape[0]] = turned[0:half].astype(BF16)
        edge[here : here + 1] = block[half : half + 1]
        edge_turned[there : there + 1] = turned[half : half + 1]


def own_green(plan, follows, green, own):
    devices, rows, half = plan.devices, plan.rows, plan.half
    partner = follows[0] == 1
    first = lax.broadcasted_iota(jnp.int32, (half, rows), 0) == 0
    for m in range(devices):
        turned = green[pl.ds(m, rows, stride=devices), :].T
        swap = jnp.broadcast_to(turned[half : half + 1], (half, rows))
        own[plan.place_of(m)] = jnp.where(first & partner, swap, turned[0:half])


def slot_choice(owners, capacity, slots):
    blocks = owners.shape[1]
    across = jnp.broadcast_to(owners[...].astype(F32), (blocks, blocks))
    first = lax.broadcasted_iota(jnp.int32, across.shape, 0)
    second = lax.broadcasted_iota(jnp.int32, across.shape, 1)
    earlier = jnp.where((across.T == across) & (first < second), 1.0, 0.0)
    slot = across[0:1] * capacity + jnp.sum(earlier, axis=0, keepdims=True)
    place = lax.broadcasted_iota(jnp.int32, (slots, blocks), 0)
    return jnp.where(place == slot.astype(jnp.int32), 1.0, 0.0)


def own_lanes(block_size):
    row = lax.broadcasted_iota(jnp.int32, (STEP, STEP * block_size), 0)
    lane = lax.broadcasted_iota(jnp.int32, (STEP, STEP * block_size), 1)
    return row == lane // block_size


def block_rows(stencil, group):
    _, block_size, cells = stencil.shape
    return stencil[group * STEP : (group + 1) * STEP].reshape(STEP * block_size, cells)


def start_blocks(loads, source, target):
    copies = []
    for group in range(source.shape[0] // STEP):
        here = pl.ds(group * STEP, STEP)
        copies.append(loads.start(source.at[here], target.at[here]))
    return copies


def project(values, stencil, chosen, need):
    mine = own_lanes(stencil.shape[1])
    each = mine.shape[1] // LANES
    tiles = []
    for group in range(stencil.shape[0] // STEP):
        rows = [values[i : i + 1] for i in range(group * each, (group + 1) * each)]
        spread = jnp.concatenate([jnp.broadcast_to(row, (STEP, LANES)) for row in rows], axis=1)
        need(group)
        spread = jnp.where(mine, spread, 0.0).astype(BF16)
        tiles.append(dot(spread, block_rows(stencil, group)))
    tiles = jnp.concatenate(tiles, axis=0)
    high = tiles.astype(BF16)
    low = (tiles - high.astype(F32)).astype(BF16)
    return dot(chosen, high) + dot(chosen, low)


def interpolate(returned, stencil, chosen, need):
    mine = own_lanes(stencil.shape[1])
    own = lax.dot_general(
        chosen, returned[...], (((0,), (0,)), ((), ())), preferred_element_type=F32
    ).astype(BF16)
    far = []
    for group in range(stencil.shape[0] // STEP):
        need(group)
        every = lax.dot_general(
            own[group * STEP : (group + 1) * STEP],
            block_rows(stencil, group),
            (((1,), (1,)), ((), ())),
            preferred_element_type=F32,
        )
        sums = jnp.sum(jnp.where(mine, every, 0.0), axis=0, keepdims=True)
        far += [sums[:, i : i + LANES] for i in range(0, mine.shape[1], LANES)]
    return jnp.concatenate(far, axis=0)


def first_tiles(capacity, owners_in, tiles_in, values_in, stencil_in, out, owners, tiles, values, stencil, tosend, ins, outs):
    slots, cells = out.shape[0], stencil.shape[2]
    loads, stores = Copies(ins), Copies(outs)
    small = [
        loads.start(owners_in, owners),
        loads.start(tiles_in, tiles),
        loads.start(values_in, values),
    ]
    blocks = start_blocks(loads, stencil_in, stencil)
    for copy in small:
        copy.wait()
    chosen = slot_choice(owners, capacity, slots)
    marks = jnp.sum(chosen * (tiles[...] + 1).astype(F32), axis=1, keepdims=True)
    tosend[:, cells:] = jnp.broadcast_to(marks, (slots, out.shape[1] - cells))
    tosend[:, :cells] = project(
        values[...].astype(F32), stencil, chosen.astype(BF16), lambda group: blocks[group].wait()
    )
    stores.start(tosend, out)
    stores.wait()


def middle_blocks(capacity, owners_in, returned_in, near_in, target_in, stencil_in, potentials, residual, out, owners, returned, near, target, stencil, tosend, ins, outs):
    loads, stores = Copies(ins), Copies(outs)
    load_owners = loads.start(owners_in, owners)
    load_returned = loads.start(returned_in, returned)
    blocks = start_blocks(loads, stencil_in, stencil)
    later = [loads.start(near_in, near), loads.start(target_in, target)]
    load_owners.wait()
    chosen = slot_choice(owners, capacity, out.shape[0]).astype(BF16)
    load_returned.wait()
    far = interpolate(returned, stencil, chosen, lambda group: blocks[group].wait())
    for copy in later:
        copy.wait()
    total = far + near[...]
    potentials[...] = total
    rounded = (total - target[...]).astype(BF16)
    residual[...] = rounded
    tosend[...] = project(rounded.astype(F32), stencil, chosen, lambda group: None)
    stores.start(tosend, out)
    stores.wait()


def last_blocks(capacity, owners_in, returned_in, near_in, stencil_in, gradient, owners, returned, near, stencil, ins):
    loads = Copies(ins)
    load_owners = loads.start(owners_in, owners)
    load_returned = loads.start(returned_in, returned)
    blocks = start_blocks(loads, stencil_in, stencil)
    last = loads.start(near_in, near)
    load_owners.wait()
    chosen = slot_choice(owners, capacity, returned.shape[0]).astype(BF16)
    load_returned.wait()
    far = interpolate(returned, stencil, chosen, lambda group: blocks[group].wait())
    last.wait()
    gradient[...] = far + near[...]


def kernel(body, plan, out_shape, scratch, scalars, operands):
    in_specs = [pl.BlockSpec(memory_space=pltpu.SMEM)] * len(scalars)
    in_specs += [pl.BlockSpec(memory_space=pltpu.VMEM)] * len(operands)
    return pl.pallas_call(
        functools.partial(body, plan),
        out_shape=out_shape,
        in_specs=in_specs,
        out_specs=jax.tree.map(lambda _: pl.BlockSpec(memory_space=pltpu.VMEM), out_shape),
        scratch_shapes=scratch,
        compiler_params=pltpu.CompilerParams(vmem_limit_bytes=WIDE),
    )(*scalars, *operands)


def streamed(
    body, plan, out_shape, out_spaces, scratch, copies, scalars, operands, grant=WIDE
):
    space = pl.ANY if grant == WIDE else pltpu.VMEM
    in_specs = [pl.BlockSpec(memory_space=pltpu.SMEM)] * len(scalars)
    in_specs += [pl.BlockSpec(memory_space=space)] * len(operands)
    semaphores = [pltpu.SemaphoreType.DMA((count,)) for count in copies]
    return pl.pallas_call(
        functools.partial(body, plan),
        out_shape=out_shape,
        in_specs=in_specs,
        out_specs=jax.tree.map(lambda space: pl.BlockSpec(memory_space=space), out_spaces),
        scratch_shapes=[*scratch, *semaphores],
        compiler_params=pltpu.CompilerParams(vmem_limit_bytes=grant),
    )(*scalars, *operands)


def held(*arrays):
    return [pltpu.VMEM(array.shape, array.dtype) for array in arrays]


def leaving_green(plan, green):
    devices, half, rows = plan.devices, plan.half, plan.rows
    pick, turn = plan.mirror_tables()
    ahead = devices // 2
    early = jax.ShapeDtypeStruct((ahead, half, rows), BF16)
    late = jax.ShapeDtypeStruct((devices - ahead, half, rows), BF16)
    line = jax.ShapeDtypeStruct((devices, rows), F32)
    return kernel(
        mirrored_green,
        plan,
        (early, late, line, line),
        [pltpu.VMEM((plan.grid, half + STEP), F32)],
        [],
        [green, jnp.asarray(pick), jnp.asarray(turn)],
    )


def staying_green(plan, green):
    devices, half, rows, per_mu = plan.devices, plan.half, plan.rows, plan.per_mu
    partner = lax.axis_index(AXES) % per_mu >= per_mu // 2
    return kernel(
        own_green,
        plan,
        jax.ShapeDtypeStruct((devices, half, rows), F32),
        [],
        [partner.astype(jnp.int32).reshape(1)],
        [green],
    )


def swap_mirrored(plan, part):
    return lax.ppermute(part, AXES, [(i, plan.devices - 1 - i) for i in range(plan.devices)])


def swap_edges(plan, edge, edge_turned):
    devices, per_mu, tile = plan.devices, plan.per_mu, plan.tile
    upper = range(tile // 2, tile)
    plain = [(devices // 2, 0)]
    plain += [(per_mu * (m - tile // 2) + per_mu // 2, per_mu * m) for m in upper]
    mirror = [(devices // 2, 0)]
    mirror += [(per_mu * (tile - 1 - m + tile // 2) + per_mu // 2, per_mu * m) for m in upper]
    for i in range(1, devices):
        low = i % per_mu
        if low < per_mu // 2 and (low or i // per_mu < tile // 2):
            mirror.append((devices - i, i))
    return lax.ppermute(edge, AXES, plain), lax.ppermute(edge_turned, AXES, mirror)


def edge_lines(plan, edges, swapped_edges):
    edge, edge_turned = edges
    edge_plain, edge_mirror = swapped_edges
    me = lax.axis_index(AXES)
    mu, part = me // plan.per_mu, me % plan.per_mu
    shared = (part == 0) & (mu >= plan.tile // 2)
    head = jnp.where(shared, edge_plain, edge) + jnp.where(me == 0, edge_turned, edge_mirror)
    return head, edge_plain + edge_mirror


def local(charges, target, stencil, near_matrix, green, block_dest, block_tile, near_offset):
    devices = lax.axis_size(AXES)
    blocks, block_size, cell_count = stencil.shape
    pair_count = near_offset.shape[1]
    capacity = 2 * blocks // devices
    slots = devices * capacity
    plan = Plan(green.shape[0], math.isqrt(cell_count), devices)
    me = lax.axis_index(AXES)
    owners = block_dest.reshape(1, blocks)
    flat = (blocks * block_size // LANES, LANES)
    steps = blocks // STEP
    forward_table = jnp.asarray(plan.forward_table())
    inverse_table = jnp.asarray(plan.inverse_table())
    twiddle = jnp.asarray(plan.column_twiddles())
    edge_forward, edge_inverse = (jnp.asarray(t) for t in plan.edge_tables())
    both, row_twiddle = (jnp.asarray(t) for t in plan.row_tables())
    origin = (me == 0).astype(jnp.int32).reshape(1)
    partner = (me % plan.per_mu >= plan.per_mu // 2).astype(jnp.int32).reshape(1)
    early, late, *edges = leaving_green(plan, green)
    spectrum_shape = jax.ShapeDtypeStruct((devices, plan.width, plan.rows), BF16)
    tall_shape = (devices, 2 * plan.half + STEP, plan.rows)
    half_steps = plan.half // STEP
    green_shape = jax.ShapeDtypeStruct((devices, plan.half + 8, plan.rows), F32)
    column_work = [
        pltpu.VMEM(spectrum_shape.shape, BF16),
        pltpu.VMEM(tall_shape, F32),
        pltpu.VMEM(tall_shape, BF16),
    ]
    work_shape = (plan.tile // plan.group, plan.tile_cols, plan.group * plan.rows)

    def exchange(values):
        return lax.all_to_all(values, AXES, split_axis=0, concat_axis=0, tiled=True)

    def to_columns(arrived, marked, grant):
        operands = [arrived, marked, forward_table, twiddle, edge_forward]
        copied = [pltpu.VMEM((slots, cell_count), F32), pltpu.VMEM((slots, 128), F32)]
        copied += held(forward_table, twiddle, edge_forward)
        wide = grant == WIDE
        return streamed(
            forward_rows if wide else resident_forward_rows,
            plan,
            spectrum_shape,
            pl.ANY,
            [
                *(copied if wide else []),
                pltpu.VMEM(work_shape, F32),
                pltpu.VMEM(spectrum_shape.shape, BF16),
            ],
            (5, devices) if wide else (devices,),
            [],
            operands,
            grant,
        )

    def along_columns(spectrum, weights):
        return streamed(
            columns,
            plan,
            spectrum_shape,
            pl.ANY,
            column_work,
            (2 * half_steps,),
            [origin],
            [spectrum, weights, both, row_twiddle],
            NARROW,
        )

    def to_rows(spectrum, marked):
        picked = streamed(
            inverse_rows,
            plan,
            jax.ShapeDtypeStruct((slots, cell_count), BF16),
            pl.ANY,
            [pltpu.VMEM(work_shape, BF16), pltpu.VMEM((slots, cell_count), BF16)],
            (1,),
            [],
            [spectrum, marked, inverse_table, twiddle, edge_inverse],
            NARROW,
        )
        return exchange(picked.reshape(devices, capacity, cell_count)).reshape(slots, cell_count)

    couple = near_matrix.reshape(blocks, pair_count, block_size, block_size)
    positions = jnp.arange(blocks, dtype=jnp.int32)[:, None] + REACH + near_offset
    charge_blocks = charges.reshape(blocks, block_size)
    sources = extended_2(charge_blocks, ((AXES, 0),), REACH)[positions]

    tiles = block_tile.reshape(1, blocks)
    values = charges.reshape(flat)
    outgoing_shape = jax.ShapeDtypeStruct((slots, cell_count + 128), F32)
    outgoing = streamed(
        first_tiles,
        capacity,
        outgoing_shape,
        pl.ANY,
        held(owners, tiles, values, stencil, outgoing_shape),
        (3 + steps, 1),
        [],
        [owners, tiles, values, stencil],
    )
    swapped_edges = swap_edges(plan, *edges)
    arrived = exchange(outgoing.reshape(devices, capacity, -1)).reshape(slots, -1)
    early = swap_mirrored(plan, early)
    arrived, late, edges, couple = lax.optimization_barrier((arrived, late, edges, couple))
    late = swap_mirrored(plan, late)
    marked = arrived
    spectrum = to_columns(arrived, marked, NARROW)
    spectrum, early = lax.optimization_barrier((spectrum, early))
    lines = edge_lines(plan, edges, swapped_edges)
    own = staying_green(plan, green)
    spectrum, couple, sources, own = lax.optimization_barrier(
        (exchange(spectrum), couple, sources, own)
    )
    green_parts = [own, early, late, *lines]
    spectrum, weights = streamed(
        first_columns,
        plan,
        (spectrum_shape, green_shape),
        (pl.ANY, pl.ANY),
        [
            *held(spectrum, green_shape, both, row_twiddle),
            *column_work,
            *held(*green_parts),
        ],
        (2 * half_steps + 2 + len(green_parts), 2 * half_steps + 1),
        [origin, partner],
        [spectrum, *green_parts, both, row_twiddle],
    )
    returned = to_rows(exchange(spectrum), marked)
    near = jnp.einsum("bkps,bks->bp", couple, sources, preferred_element_type=F32)
    near, target = near.reshape(flat), target.reshape(flat)
    outgoing_shape = jax.ShapeDtypeStruct((slots, cell_count), F32)
    potentials, residual, outgoing = streamed(
        middle_blocks,
        capacity,
        (
            jax.ShapeDtypeStruct(flat, F32),
            jax.ShapeDtypeStruct(flat, BF16),
            outgoing_shape,
        ),
        (pltpu.VMEM, pltpu.VMEM, pl.ANY),
        held(owners, returned, near, target, stencil, outgoing_shape),
        (4 + steps, 1),
        [],
        [owners, returned, near, target, stencil],
    )

    arrived = exchange(outgoing.reshape(devices, capacity, -1)).reshape(slots, -1)
    residual = residual.reshape(blocks, block_size)
    terms = jnp.einsum("bkps,bp->bks", couple, residual, preferred_element_type=F32)
    spectrum = exchange(to_columns(arrived, marked, NARROW))
    spectrum, terms = lax.optimization_barrier((spectrum, terms))
    spectrum = exchange(along_columns(spectrum, weights))
    extended = jnp.zeros((blocks + 2 * REACH, block_size), F32)
    extended = extended.at[positions.reshape(-1)].add(terms.reshape(-1, block_size))
    rims = jnp.concatenate([extended[:REACH], extended[blocks + REACH :]], axis=0)
    neighbour = extended_2(rims, ((AXES, 0),), REACH)
    own_part = extended[REACH : blocks + REACH]
    own_part = own_part.at[:REACH].add(neighbour[:REACH])
    own_part = own_part.at[blocks - REACH :].add(neighbour[3 * REACH :])
    returned = to_rows(spectrum, marked)
    near = own_part.reshape(flat)
    gradient = streamed(
        last_blocks,
        capacity,
        jax.ShapeDtypeStruct(flat, F32),
        pltpu.VMEM,
        held(owners, returned, near, stencil),
        (3 + steps,),
        [],
        [owners, returned, near, stencil],
    )
    return (potentials.reshape(-1), gradient.reshape(-1))


def solution(mesh):
    rows = P(AXES)
    return jax.shard_map(
        local,
        mesh=mesh,
        in_specs=(rows, rows, rows, rows, P(None, AXES), rows, rows, rows),
        out_specs=(rows, rows),
        check_vma=False,
    )
```

```python
import functools
import math

import jax
import jax.numpy as jnp
import numpy as np
from jax import lax
from jax.experimental import pallas as pl
from jax.experimental.pallas import tpu as pltpu
from jax.sharding import PartitionSpec as P

REACH = 8
AXES = ("panel", "slab")
BF16 = jnp.bfloat16
F32 = jnp.float32
WIDE = 56 * 1024 * 1024
NARROW = 24 * 1024 * 1024
STEP = 16
LANES = 128


def extended_2(cells, sides, width):
    for axis, dim in sides:
        count = lax.axis_size(axis)
        ends = count - 1
        head = lax.slice_in_dim(cells, 0, width, axis=dim)
        tail = lax.slice_in_dim(cells, cells.shape[dim] - width, cells.shape[dim], axis=dim)
        cells = jnp.concatenate(
            [
                lax.ppermute(tail, axis, [(i, (i + 1) % count) for i in range(ends)]),
                cells,
                lax.ppermute(head, axis, [((i + 1) % count, i) for i in range(ends)]),
            ],
            axis=dim,
        )
    return cells


def split(table):
    high = table.astype(jnp.bfloat16)
    return np.stack([high, (table - high.astype(np.float64)).astype(jnp.bfloat16)])


class Plan:
    def __init__(self, grid, tile, devices):
        self.grid, self.tile, self.devices = grid, tile, devices
        self.tile_cols = grid // tile
        self.rows = grid // devices
        self.width = grid // devices
        self.half = self.width // 2
        self.per_mu = devices // tile
        self.kappas = self.tile_cols // 2
        self.group = max(1, min(tile, 2 * 128 // self.rows))

    def factors(self):
        outer = 1 << ((self.devices.bit_length() - 1) // 2)
        return outer, self.devices // outer

    def low_part(self, index):
        outer, inner = self.factors()
        return index // inner + outer * (index % inner)

    def place_of(self, low):
        outer, inner = self.factors()
        return (low % outer) * inner + low // outer

    def place(self, position, mu):
        part, j = divmod(position, self.width)
        device = self.per_mu * mu + part
        if j < self.half:
            return device, j, 1.0
        return self.devices - 1 - device, j - self.half, -1.0

    def kappa(self):
        out = []
        for position in range(self.kappas):
            part, j = divmod(position, self.width)
            if j >= self.half:
                j = self.half + (self.half - (j - self.half)) % self.half
            out.append(self.width * part + j)
        return np.array(out)

    def forward_table(self):
        angle = 2 * np.pi * np.outer(self.kappa(), np.arange(self.tile_cols)) / self.tile_cols
        sine = -np.sin(angle)
        sine[0] = (-1.0) ** np.arange(self.tile_cols)
        return split(np.concatenate([np.cos(angle), sine]))

    def inverse_table(self):
        angle = 2 * np.pi * np.outer(np.arange(self.tile_cols), self.kappa()) / self.tile_cols
        cosine, sine = 2 * np.cos(angle), -2 * np.sin(angle)
        cosine[:, 0] = 1.0
        sine[:, 0] = (-1.0) ** np.arange(self.tile_cols)
        return split(np.concatenate([cosine, sine], axis=1))

    def column_twiddles(self):
        angle = 2 * np.pi * self.kappa() / self.grid
        full = np.broadcast_to(angle[:, None], (self.kappas, self.rows))
        return np.stack([np.cos(full), np.sin(full)]).astype(np.float32)

    def edge_tables(self):
        n, m = self.tile, self.tile // 2
        cells = np.arange(n)
        forward, inverse = np.zeros((2 * n, 2 * n)), np.zeros((2 * n, 2 * n))
        forward[0, :n], forward[n, :n] = 1.0, (-1.0) ** cells
        inverse[:n, 0], inverse[:n, n] = 1.0, (-1.0) ** cells
        for mu in range(1, m):
            angle = 2 * np.pi * cells * mu / n
            forward[mu, :n], forward[n + mu, :n] = np.cos(angle), -np.sin(angle)
            inverse[:n, mu], inverse[:n, n + mu] = 2 * np.cos(angle), -2 * np.sin(angle)
        for nu in range(m):
            angle = 2 * np.pi * cells * (1 + 2 * nu) / (2 * n)
            forward[m + nu, n:], forward[n + m + nu, n:] = np.cos(angle), -np.sin(angle)
            inverse[n:, m + nu], inverse[n:, n + m + nu] = 2 * np.cos(angle), -2 * np.sin(angle)
        return forward.astype(np.float32), inverse.astype(np.float32)

    def row_tables(self):
        n = self.rows
        angle = 2 * np.pi * (np.outer(np.arange(n), np.arange(n)) % n) / n
        both = split(np.concatenate([np.cos(angle), np.sin(angle)], axis=1))
        low = [self.low_part(index) for index in range(self.devices)]
        angle = 2 * np.pi * np.outer(low, np.arange(n)) / self.grid
        return both.reshape(2 * n, 2 * n), np.stack([np.cos(angle), np.sin(angle)]).astype(np.float32)

    def mirror_tables(self):
        pick = np.zeros((self.half + STEP, self.width))
        pick[self.half, 0] = 1.0
        for i in range(self.half):
            pick[i, self.width - i if i else self.half] = 1.0
        n = self.rows
        first, rest = np.zeros((n, n)), np.zeros((n, n))
        for i in range(n):
            first[(n - i) % n, i] = 1.0
            rest[n - 1 - i, i] = 1.0
        return pick.T.astype(jnp.bfloat16), np.stack([first, rest]).astype(jnp.bfloat16)


def transform(points, sign):
    count = len(points)
    if count == 1:
        return points
    even, odd = transform(points[0::2], sign), transform(points[1::2], sign)
    low, high = [], []
    for k in range(count // 2):
        (er, ei), (re, im) = even[k], odd[k]
        if 4 * k == count:
            re, im = (-im, re) if sign > 0 else (im, -re)
        elif 8 * k == count or 8 * k == 3 * count:
            root = math.sqrt(0.5)
            if 8 * k == count:
                re, im = (re - sign * im) * root, (im + sign * re) * root
            else:
                re, im = (-re - sign * im) * root, (sign * re - im) * root
        elif k:
            c, s = math.cos(2 * math.pi * k / count), sign * math.sin(2 * math.pi * k / count)
            re, im = re * c - im * s, im * c + re * s
        low.append((er + re, ei + im))
        high.append((er - re, ei - im))
    return low + high


def dot(a, b):
    return jnp.dot(a, b, preferred_element_type=F32)


def slot_tiles(marks, plan):
    number = marks.astype(jnp.int32) - 1
    shift = plan.tile_cols.bit_length() - 1
    return number & (plan.tile_cols - 1), number >> shift


def slot_mask(tile_row, plan):
    mine = tile_row[:, : plan.rows]
    lane = lax.broadcasted_iota(jnp.int32, mine.shape, 1) // plan.tile
    mask = (mine == lane).astype(F32)
    return jnp.concatenate([mask] * plan.group, axis=1) > 0.5


class Copies:
    def __init__(self, semaphores):
        self.semaphores, self.started = semaphores, []

    def start(self, source, target):
        copy = pltpu.make_async_copy(source, target, self.semaphores.at[len(self.started)])
        copy.start()
        self.started.append(copy)
        return copy

    def wait(self):
        for copy in self.started:
            copy.wait()


class Present:
    def wait(self):
        pass


def bring(loads, source, target):
    if target is None:
        return source, Present()
    return target, loads.start(source, target)


def cell_lanes(plan):
    cells, span = plan.tile * plan.tile, plan.group * plan.rows
    cell = lax.broadcasted_iota(jnp.int32, (cells, span), 0)
    lane = lax.broadcasted_iota(jnp.int32, (cells, span), 1)
    differs = (cell & (plan.tile - 1)) - lane // plan.rows
    return jnp.where(cell // plan.tile == (lane & (plan.tile - 1)), differs, -plan.tile)


def spread_lanes(plan, lanes, chunk):
    return jnp.where(lanes == chunk * plan.group, 1.0, 0.0).astype(BF16)


def powers(cosine, sine, count):
    out = [None, (cosine, sine)]
    for k in range(2, count):
        (c, s), (d, t) = out[k // 2], out[k - k // 2]
        out.append((c * d - s * t, s * d + c * t))
    return out


def resident_forward_rows(plan, values, marked, table, twiddle, edge, out, work, lines, outs):
    none = [None] * 5
    forward_rows(plan, values, marked, table, twiddle, edge, out, *none, work, lines, None, outs)


def forward_rows(plan, values_in, marked_in, table_in, twiddle_in, edge_in, out, values, marked, table, twiddle, edge, work, lines, ins, outs):
    tile, rows, group, half = plan.tile, plan.rows, plan.group, plan.half
    slots, cells = values_in.shape[0], tile * tile
    loads = Copies(ins)
    marked, load_marks = bring(loads, marked_in.at[:, cells:], marked)
    table, load_table = bring(loads, table_in, table)
    values, load_values = bring(loads, values_in.at[:, :cells], values)
    twiddle, load_twiddle = bring(loads, twiddle_in, twiddle)
    edge, load_edge = bring(loads, edge_in, edge)
    lanes = cell_lanes(plan)
    load_marks.wait()
    marks = marked[...]
    _, tile_row = slot_tiles(marks, plan)
    mask = slot_mask(tile_row, plan)
    tile_col, _ = slot_tiles(marks.T[0:1, :], plan)
    place = lax.broadcasted_iota(jnp.int32, (plan.tile_cols, slots), 0)
    chosen = (place == tile_col).astype(F32).astype(BF16)
    load_table.wait()
    weights = dot(table[0], chosen).astype(BF16)
    weights_low = dot(table[1], chosen).astype(BF16)
    load_values.wait()
    exact = values[...]
    high = exact.astype(BF16)
    low = (exact - high.astype(F32)).astype(BF16)
    for chunk in range(tile // group):
        spread = spread_lanes(plan, lanes, chunk)
        high_part = jnp.where(mask, dot(high, spread), 0.0).astype(BF16)
        low_part = jnp.where(mask, dot(low, spread), 0.0).astype(BF16)
        work[chunk] = (
            dot(weights, high_part) + dot(weights, low_part) + dot(weights_low, high_part)
        )
    load_twiddle.wait()
    load_edge.wait()

    def piece(cell, start, size):
        at = (cell % group) * rows
        return work[cell // group, start : start + size, at : at + rows]

    ends = [piece(cell, 0, 8)[0:1] for cell in range(tile)]
    ends += [piece(cell, plan.kappas, 8)[0:1] for cell in range(tile)]
    shared = jnp.dot(
        edge[...],
        jnp.concatenate(ends, axis=0),
        precision=lax.Precision.HIGHEST,
        preferred_element_type=F32,
    )
    first = lax.broadcasted_iota(jnp.int32, (STEP, rows), 0) == 0
    stores = Copies(outs)
    for start in range(0, plan.kappas, STEP):
        at = slice(start, start + STEP)
        turns = powers(twiddle[0, at], twiddle[1, at], tile)
        points = []
        for cell in range(tile):
            re, im = piece(cell, start, STEP), piece(cell, plan.kappas + start, STEP)
            if cell:
                c, s = turns[cell]
                re, im = re * c + im * s, im * c - re * s
            points.append((re, im))
        for mu, (re, im) in enumerate(transform(points, -1)):
            if start == 0:
                re = jnp.where(first, shared[mu : mu + 1], re)
                im = jnp.where(first, shared[tile + mu : tile + mu + 1], im)
            device, row, sign = plan.place(start, mu)
            lines[device, row : row + STEP] = re.astype(BF16)
            lines[device, half + row : half + row + STEP] = (im * sign).astype(BF16)
            if row + STEP == half:
                stores.start(lines.at[device], out.at[device])
    stores.wait()


def inverse_rows(plan, spectrum, marked, table, twiddle, edge, out, work, picked, outs):
    tile, rows, group, half = plan.tile, plan.rows, plan.group, plan.half
    slots, cells = marked.shape[0], tile * tile
    lanes = cell_lanes(plan)
    tile_col, tile_row = slot_tiles(marked[:, cells:], plan)
    mask = slot_mask(tile_row, plan)
    place = lax.broadcasted_iota(jnp.int32, (slots, plan.tile_cols), 1)
    chosen = (place == tile_col[:, 0:1]).astype(F32).astype(BF16)
    first = lax.broadcasted_iota(jnp.int32, (STEP, rows), 0) == 0
    for row in range(0, half, STEP):
        if row == 0:
            ends = [spectrum[plan.per_mu * mu, 0:STEP].astype(F32)[0:1] for mu in range(tile)]
            ends += [
                spectrum[plan.per_mu * mu, half : half + STEP].astype(F32)[0:1] for mu in range(tile)
            ]
            shared = jnp.dot(
                edge[...],
                jnp.concatenate(ends, axis=0),
                precision=lax.Precision.HIGHEST,
                preferred_element_type=F32,
            )
        for start in range(0, plan.kappas, STEP):
            if plan.place(start, 0)[1] != row:
                continue
            points = []
            for mu in range(tile):
                device, _, sign = plan.place(start, mu)
                re = spectrum[device, row : row + STEP].astype(F32)
                im = spectrum[device, half + row : half + row + STEP].astype(F32) * sign
                points.append((re, im))
            at = slice(start, start + STEP)
            second = slice(plan.kappas + start, plan.kappas + start + STEP)
            turns = powers(twiddle[0, at], twiddle[1, at], tile)
            for cell, (re, im) in enumerate(transform(points, 1)):
                if cell:
                    c, s = turns[cell]
                    re, im = re * c - im * s, im * c + re * s
                if start == 0:
                    re = jnp.where(first, shared[cell : cell + 1], re)
                    im = jnp.where(first, shared[tile + cell : tile + cell + 1], im)
                here = (cell % group) * rows
                work[cell // group, at, here : here + rows] = re.astype(BF16)
                work[cell // group, second, here : here + rows] = im.astype(BF16)
    weights = dot(chosen, table[0]).astype(BF16)
    weights_low = dot(chosen, table[1]).astype(BF16)
    total = jnp.zeros(picked.shape, F32)
    for chunk in range(tile // group):
        field = dot(weights, work[chunk]) + dot(weights_low, work[chunk])
        field = jnp.where(mask, field, 0.0).astype(BF16)
        total = total + lax.dot_general(
            field,
            spread_lanes(plan, lanes, chunk),
            (((1,), (1,)), ((), ())),
            preferred_element_type=F32,
        )
    picked[...] = total.astype(BF16)
    stores = Copies(outs)
    stores.start(picked, out)
    stores.wait()


def turn_by(point, cosine, sine):
    re, im = point
    return re * cosine - im * sine, im * cosine + re * sine


def columns(plan, origin, spectrum, green, both, twiddle, out, result, work, rows16, outs):
    stores = Copies(outs)
    every_column(
        plan, origin, [], spectrum, green, both, twiddle, lambda: None, stores, out,
        result, work, rows16,
    )
    stores.wait()


def start_columns(plan, loads, spectrum_in, spectrum, both_in, both, twiddle_in, twiddle):
    arriving = []
    for start in range(0, plan.half, STEP):
        for at in (start, plan.half + start):
            here = pl.ds(at, STEP)
            arriving.append(loads.start(spectrum_in.at[:, here, :], spectrum.at[:, here, :]))
        if start == 0:
            arriving.append(loads.start(twiddle_in, twiddle))
            arriving.append(loads.start(both_in, both))
    return arriving


def every_column(plan, origin, arriving, spectrum, green, both, twiddle, need_green, stores, out, result, work, rows16):
    devices, rows, half = plan.devices, plan.rows, plan.half
    outer, inner = plan.factors()
    holds_edge = origin[0] == 1
    tall = 2 * half + STEP
    groups = [(start, half + start, STEP) for start in range(0, half, STEP)]
    groups.insert(1, (2 * half, 2 * half + 8, 8))
    top = (lax.broadcasted_iota(jnp.int32, (STEP, rows), 0) == 0) & holds_edge

    def constant(cell, low, sign):
        angle = 2 * math.pi * cell * low / devices
        return math.cos(angle), sign * math.sin(angle)

    def source(s, start):
        if start == 2 * half:
            shared = spectrum[s, half : half + STEP].astype(F32)
            return jnp.where(top, shared, 0.0)[0:8], jnp.zeros((8, rows), F32)
        re = spectrum[s, start : start + STEP].astype(F32)
        im = spectrum[s, half + start : half + start + STEP].astype(F32)
        return re, (jnp.where(top, 0.0, im) if start == 0 else im)

    arriving = list(arriving)
    for first, second, size in groups:
        at_re, at_im = slice(first, first + size), slice(second, second + size)
        if size == STEP:
            for copy in arriving[: 4 if first == 0 else 2]:
                copy.wait()
            arriving = arriving[4 if first == 0 else 2 :]
        for b in range(inner):
            points = [source(a * inner + b, first) for a in range(outer)]
            for low, point in enumerate(transform(points, -1)):
                if low and b:
                    point = turn_by(point, *constant(b, low, -1))
                work[low * inner + b, at_re], work[low * inner + b, at_im] = point
        for low in range(outer):
            base = low * inner
            points = [(work[base + b, at_re], work[base + b, at_im]) for b in range(inner)]
            for high, point in enumerate(transform(points, -1)):
                c, s = (twiddle[part, base + high : base + high + 1] for part in (0, 1))
                re, im = turn_by(point, c, -s)
                if size == 8:
                    both_parts = jnp.concatenate([re, im], axis=0)
                    rows16[base + high, 2 * half : tall] = both_parts.astype(BF16)
                else:
                    rows16[base + high, at_re] = re.astype(BF16)
                    rows16[base + high, at_im] = im.astype(BF16)
    need_green()
    batch = 4
    spans = [(0, half, 2 * half), (2 * half, 2 * half + 8, tall)]

    def product(values):
        flat = values.reshape(batch * tall, rows)
        twice = jnp.concatenate([flat, flat], axis=1)
        return dot(twice, both[...]).reshape(batch, tall, 2 * rows)

    def middle(i, carry):
        at = pl.ds(i * batch, batch)
        u = product(rows16[at])
        g = green[at]
        parts = []
        for (a, b, c), here in zip(spans, (g[:, :half], g[:, half:])):
            parts.append((u[:, a:b, :rows] + u[:, b:c, rows:]) * here)
            parts.append((u[:, b:c, :rows] - u[:, a:b, rows:]) * here)
        u = product(jnp.concatenate(parts, axis=1).astype(BF16))
        turn_c, turn_s = twiddle[0, at][:, None, :], twiddle[1, at][:, None, :]
        for a, b, c in spans:
            re = u[:, a:b, :rows] - u[:, b:c, rows:]
            im = u[:, b:c, :rows] + u[:, a:b, rows:]
            work[at, a:b], work[at, b:c] = turn_by((re, im), turn_c, turn_s)
        return carry

    lax.fori_loop(0, devices // batch, middle, 0, unroll=8)

    for first, second, size in [groups[1], groups[0], *groups[2:]]:
        at_re, at_im = slice(first, first + size), slice(second, second + size)
        for low in range(outer):
            base = low * inner
            points = [(work[base + high, at_re], work[base + high, at_im]) for high in range(inner)]
            for b, point in enumerate(transform(points, 1)):
                if low and b:
                    point = turn_by(point, *constant(b, low, 1))
                work[base + b, at_re], work[base + b, at_im] = point
        for b in range(inner):
            points = [
                (work[low * inner + b, at_re], work[low * inner + b, at_im])
                for low in range(outer)
            ]
            for a, (re, im) in enumerate(transform(points, 1)):
                s = a * inner + b
                if size == 8:
                    work[s, at_re] = re
                    continue
                if first == 0:
                    im = jnp.where(top, work[s, 2 * half : 2 * half + STEP], im)
                result[s, at_re] = re.astype(BF16)
                result[s, at_im] = im.astype(BF16)
        if size == STEP:
            for at in (first, second):
                here = pl.ds(at, STEP)
                stores.start(result.at[:, here, :], out.at[:, here, :])


def first_columns(plan, origin, follows, shares, spectrum_in, own_in, early_in, late_in, edge_in, turned_in, plain_in, mirror_in, both_in, twiddle_in, out, weights_out, spectrum, green, both, twiddle, result, work, rows16, own, early, late, edge, turned, plain, mirror, ins, outs):
    half, rows, ahead = plan.half, plan.rows, early.shape[0]
    loads, stores = Copies(ins), Copies(outs)
    arriving = start_columns(plan, loads, spectrum_in, spectrum, both_in, both, twiddle_in, twiddle)
    parts = [(own_in, own), (early_in, early), (late_in, late)]
    parts += [(edge_in, edge), (turned_in, turned), (plain_in, plain), (mirror_in, mirror)]
    parts = [loads.start(source, target) for source, target in parts]

    def need_green():
        for copy in parts:
            copy.wait()
        scale = 0.5 / (plan.grid * plan.grid)
        extra = plain[...] + mirror[...]
        shared, at_origin = shares[0] == 1, origin[0] == 1
        head = jnp.where(shared, plain[...], edge[...])
        head = head + jnp.where(at_origin, turned[...], mirror[...])
        replaced = lax.broadcasted_iota(jnp.int32, (half, rows), 0) == 0
        replaced = replaced & (follows[0] == 0)
        top = lax.broadcasted_iota(jnp.int32, (8, rows), 0) == 0
        for s in range(plan.devices):
            received = early[s] if s < ahead else late[s - ahead]
            total = own[s] + received.astype(F32)
            total = jnp.where(replaced, jnp.broadcast_to(head[s : s + 1], total.shape), total)
            green[s, 0:half] = total * scale
            second = jnp.broadcast_to(extra[s : s + 1], top.shape)
            green[s, half : half + 8] = jnp.where(top, second, 0.0) * scale
        stores.start(green, weights_out)

    every_column(
        plan, origin, arriving, spectrum, green, both, twiddle, need_green, stores, out,
        result, work, rows16,
    )
    stores.wait()


def mirrored_green(plan, green, pick, turn, early, late, edge, edge_turned, picked):
    devices, rows, half = plan.devices, plan.rows, plan.half
    picked[...] = dot(green[...].astype(BF16), pick[...])
    for m in range(devices):
        block = picked[pl.ds(m, rows, stride=devices), :].T
        turned = dot(block.astype(BF16), turn[0 if m == 0 else 1])
        here, there = plan.place_of(m), plan.place_of((devices - m) % devices)
        if there < early.shape[0]:
            early[there] = turned[0:half].astype(BF16)
        else:
            late[there - early.shape[0]] = turned[0:half].astype(BF16)
        edge[here : here + 1] = block[half : half + 1]
        edge_turned[there : there + 1] = turned[half : half + 1]


def own_green(plan, follows, green, own):
    devices, rows, half = plan.devices, plan.rows, plan.half
    partner = follows[0] == 1
    first = lax.broadcasted_iota(jnp.int32, (half, rows), 0) == 0
    for m in range(devices):
        turned = green[pl.ds(m, rows, stride=devices), :].T
        swap = jnp.broadcast_to(turned[half : half + 1], (half, rows))
        own[plan.place_of(m)] = jnp.where(first & partner, swap, turned[0:half])


def slot_choice(owners, capacity, slots):
    blocks = owners.shape[1]
    across = jnp.broadcast_to(owners[...].astype(F32), (blocks, blocks))
    first = lax.broadcasted_iota(jnp.int32, across.shape, 0)
    second = lax.broadcasted_iota(jnp.int32, across.shape, 1)
    earlier = jnp.where((across.T == across) & (first < second), 1.0, 0.0)
    slot = across[0:1] * capacity + jnp.sum(earlier, axis=0, keepdims=True)
    place = lax.broadcasted_iota(jnp.int32, (slots, blocks), 0)
    return jnp.where(place == slot.astype(jnp.int32), 1.0, 0.0)


def own_lanes(block_size):
    row = lax.broadcasted_iota(jnp.int32, (STEP, STEP * block_size), 0)
    lane = lax.broadcasted_iota(jnp.int32, (STEP, STEP * block_size), 1)
    return row == lane // block_size


def block_rows(stencil, group):
    _, block_size, cells = stencil.shape
    return stencil[group * STEP : (group + 1) * STEP].reshape(STEP * block_size, cells)


def start_blocks(loads, source, target):
    copies = []
    for group in range(source.shape[0] // STEP):
        here = pl.ds(group * STEP, STEP)
        copies.append(loads.start(source.at[here], target.at[here]))
    return copies


def project(values, stencil, chosen, need):
    mine = own_lanes(stencil.shape[1])
    each = mine.shape[1] // LANES
    tiles = []
    for group in range(stencil.shape[0] // STEP):
        rows = [values[i : i + 1] for i in range(group * each, (group + 1) * each)]
        spread = jnp.concatenate([jnp.broadcast_to(row, (STEP, LANES)) for row in rows], axis=1)
        need(group)
        spread = jnp.where(mine, spread, 0.0).astype(BF16)
        tiles.append(dot(spread, block_rows(stencil, group)))
    tiles = jnp.concatenate(tiles, axis=0)
    high = tiles.astype(BF16)
    low = (tiles - high.astype(F32)).astype(BF16)
    return dot(chosen, high) + dot(chosen, low)


def interpolate(returned, stencil, chosen, need):
    mine = own_lanes(stencil.shape[1])
    own = lax.dot_general(
        chosen, returned[...], (((0,), (0,)), ((), ())), preferred_element_type=F32
    ).astype(BF16)
    far = []
    for group in range(stencil.shape[0] // STEP):
        need(group)
        every = lax.dot_general(
            own[group * STEP : (group + 1) * STEP],
            block_rows(stencil, group),
            (((1,), (1,)), ((), ())),
            preferred_element_type=F32,
        )
        sums = jnp.sum(jnp.where(mine, every, 0.0), axis=0, keepdims=True)
        far += [sums[:, i : i + LANES] for i in range(0, mine.shape[1], LANES)]
    return jnp.concatenate(far, axis=0)


def first_tiles(capacity, owners_in, tiles_in, values_in, stencil_in, out, owners, tiles, values, stencil, tosend, ins, outs):
    slots, cells = out.shape[0], stencil.shape[2]
    loads, stores = Copies(ins), Copies(outs)
    small = [
        loads.start(owners_in, owners),
        loads.start(tiles_in, tiles),
        loads.start(values_in, values),
    ]
    blocks = start_blocks(loads, stencil_in, stencil)
    for copy in small:
        copy.wait()
    chosen = slot_choice(owners, capacity, slots)
    marks = jnp.sum(chosen * (tiles[...] + 1).astype(F32), axis=1, keepdims=True)
    tosend[:, cells:] = jnp.broadcast_to(marks, (slots, out.shape[1] - cells))
    tosend[:, :cells] = project(
        values[...].astype(F32), stencil, chosen.astype(BF16), lambda group: blocks[group].wait()
    )
    stores.start(tosend, out)
    stores.wait()


def middle_blocks(capacity, owners_in, returned_in, near_in, target_in, stencil_in, potentials, residual, out, owners, returned, near, target, stencil, tosend, ins, outs):
    loads, stores = Copies(ins), Copies(outs)
    load_owners = loads.start(owners_in, owners)
    load_returned = loads.start(returned_in, returned)
    blocks = start_blocks(loads, stencil_in, stencil)
    later = [loads.start(near_in, near), loads.start(target_in, target)]
    load_owners.wait()
    chosen = slot_choice(owners, capacity, out.shape[0]).astype(BF16)
    load_returned.wait()
    far = interpolate(returned, stencil, chosen, lambda group: blocks[group].wait())
    for copy in later:
        copy.wait()
    total = far + near[...]
    potentials[...] = total
    rounded = (total - target[...]).astype(BF16)
    residual[...] = rounded
    tosend[...] = project(rounded.astype(F32), stencil, chosen, lambda group: None)
    stores.start(tosend, out)
    stores.wait()


def last_blocks(capacity, owners_in, returned_in, near_in, stencil_in, gradient, owners, returned, near, stencil, ins):
    loads = Copies(ins)
    load_owners = loads.start(owners_in, owners)
    load_returned = loads.start(returned_in, returned)
    blocks = start_blocks(loads, stencil_in, stencil)
    last = loads.start(near_in, near)
    load_owners.wait()
    chosen = slot_choice(owners, capacity, returned.shape[0]).astype(BF16)
    load_returned.wait()
    far = interpolate(returned, stencil, chosen, lambda group: blocks[group].wait())
    last.wait()
    gradient[...] = far + near[...]


def kernel(body, plan, out_shape, scratch, scalars, operands):
    in_specs = [pl.BlockSpec(memory_space=pltpu.SMEM)] * len(scalars)
    in_specs += [pl.BlockSpec(memory_space=pltpu.VMEM)] * len(operands)
    return pl.pallas_call(
        functools.partial(body, plan),
        out_shape=out_shape,
        in_specs=in_specs,
        out_specs=jax.tree.map(lambda _: pl.BlockSpec(memory_space=pltpu.VMEM), out_shape),
        scratch_shapes=scratch,
        compiler_params=pltpu.CompilerParams(vmem_limit_bytes=WIDE),
    )(*scalars, *operands)


def streamed(
    body, plan, out_shape, out_spaces, scratch, copies, scalars, operands, grant=WIDE
):
    space = pl.ANY if grant == WIDE else pltpu.VMEM
    in_specs = [pl.BlockSpec(memory_space=pltpu.SMEM)] * len(scalars)
    in_specs += [pl.BlockSpec(memory_space=space)] * len(operands)
    semaphores = [pltpu.SemaphoreType.DMA((count,)) for count in copies]
    return pl.pallas_call(
        functools.partial(body, plan),
        out_shape=out_shape,
        in_specs=in_specs,
        out_specs=jax.tree.map(lambda space: pl.BlockSpec(memory_space=space), out_spaces),
        scratch_shapes=[*scratch, *semaphores],
        compiler_params=pltpu.CompilerParams(vmem_limit_bytes=grant),
    )(*scalars, *operands)


def held(*arrays):
    return [pltpu.VMEM(array.shape, array.dtype) for array in arrays]


def leaving_green(plan, green):
    devices, half, rows = plan.devices, plan.half, plan.rows
    pick, turn = plan.mirror_tables()
    ahead = devices // 2
    early = jax.ShapeDtypeStruct((ahead, half, rows), BF16)
    late = jax.ShapeDtypeStruct((devices - ahead, half, rows), BF16)
    line = jax.ShapeDtypeStruct((devices, rows), F32)
    return kernel(
        mirrored_green,
        plan,
        (early, late, line, line),
        [pltpu.VMEM((plan.grid, half + STEP), F32)],
        [],
        [green, jnp.asarray(pick), jnp.asarray(turn)],
    )


def staying_green(plan, green):
    devices, half, rows, per_mu = plan.devices, plan.half, plan.rows, plan.per_mu
    partner = lax.axis_index(AXES) % per_mu >= per_mu // 2
    return kernel(
        own_green,
        plan,
        jax.ShapeDtypeStruct((devices, half, rows), F32),
        [],
        [partner.astype(jnp.int32).reshape(1)],
        [green],
    )


def swap_mirrored(plan, part):
    return lax.ppermute(part, AXES, [(i, plan.devices - 1 - i) for i in range(plan.devices)])


def swap_edges(plan, edge, edge_turned):
    devices, per_mu, tile = plan.devices, plan.per_mu, plan.tile
    upper = range(tile // 2, tile)
    plain = [(devices // 2, 0)]
    plain += [(per_mu * (m - tile // 2) + per_mu // 2, per_mu * m) for m in upper]
    mirror = [(devices // 2, 0)]
    mirror += [(per_mu * (tile - 1 - m + tile // 2) + per_mu // 2, per_mu * m) for m in upper]
    for i in range(1, devices):
        low = i % per_mu
        if low < per_mu // 2 and (low or i // per_mu < tile // 2):
            mirror.append((devices - i, i))
    return lax.ppermute(edge, AXES, plain), lax.ppermute(edge_turned, AXES, mirror)


def local(charges, target, stencil, near_matrix, green, block_dest, block_tile, near_offset):
    devices = lax.axis_size(AXES)
    blocks, block_size, cell_count = stencil.shape
    pair_count = near_offset.shape[1]
    capacity = 2 * blocks // devices
    slots = devices * capacity
    plan = Plan(green.shape[0], math.isqrt(cell_count), devices)
    me = lax.axis_index(AXES)
    owners = block_dest.reshape(1, blocks)
    flat = (blocks * block_size // LANES, LANES)
    steps = blocks // STEP
    forward_table = jnp.asarray(plan.forward_table())
    inverse_table = jnp.asarray(plan.inverse_table())
    twiddle = jnp.asarray(plan.column_twiddles())
    edge_forward, edge_inverse = (jnp.asarray(t) for t in plan.edge_tables())
    both, row_twiddle = (jnp.asarray(t) for t in plan.row_tables())
    origin = (me == 0).astype(jnp.int32).reshape(1)
    shares = (me % plan.per_mu == 0) & (me // plan.per_mu >= plan.tile // 2)
    shares = shares.astype(jnp.int32).reshape(1)
    partner = (me % plan.per_mu >= plan.per_mu // 2).astype(jnp.int32).reshape(1)
    early, late, *edges = leaving_green(plan, green)
    spectrum_shape = jax.ShapeDtypeStruct((devices, plan.width, plan.rows), BF16)
    tall_shape = (devices, 2 * plan.half + STEP, plan.rows)
    half_steps = plan.half // STEP
    green_shape = jax.ShapeDtypeStruct((devices, plan.half + 8, plan.rows), F32)
    column_work = [
        pltpu.VMEM(spectrum_shape.shape, BF16),
        pltpu.VMEM(tall_shape, F32),
        pltpu.VMEM(tall_shape, BF16),
    ]
    work_shape = (plan.tile // plan.group, plan.tile_cols, plan.group * plan.rows)

    def exchange(values):
        return lax.all_to_all(values, AXES, split_axis=0, concat_axis=0, tiled=True)

    def to_columns(arrived, marked, grant):
        operands = [arrived, marked, forward_table, twiddle, edge_forward]
        copied = [pltpu.VMEM((slots, cell_count), F32), pltpu.VMEM((slots, 128), F32)]
        copied += held(forward_table, twiddle, edge_forward)
        wide = grant == WIDE
        return streamed(
            forward_rows if wide else resident_forward_rows,
            plan,
            spectrum_shape,
            pl.ANY,
            [
                *(copied if wide else []),
                pltpu.VMEM(work_shape, F32),
                pltpu.VMEM(spectrum_shape.shape, BF16),
            ],
            (5, devices) if wide else (devices,),
            [],
            operands,
            grant,
        )

    def along_columns(spectrum, weights):
        return streamed(
            columns,
            plan,
            spectrum_shape,
            pl.ANY,
            column_work,
            (2 * half_steps,),
            [origin],
            [spectrum, weights, both, row_twiddle],
            NARROW,
        )

    def to_rows(spectrum, marked):
        picked = streamed(
            inverse_rows,
            plan,
            jax.ShapeDtypeStruct((slots, cell_count), BF16),
            pl.ANY,
            [pltpu.VMEM(work_shape, BF16), pltpu.VMEM((slots, cell_count), BF16)],
            (1,),
            [],
            [spectrum, marked, inverse_table, twiddle, edge_inverse],
            NARROW,
        )
        return exchange(picked.reshape(devices, capacity, cell_count)).reshape(slots, cell_count)

    couple = near_matrix.reshape(blocks, pair_count, block_size, block_size)
    positions = jnp.arange(blocks, dtype=jnp.int32)[:, None] + REACH + near_offset
    charge_blocks = charges.reshape(blocks, block_size)
    sources = extended_2(charge_blocks, ((AXES, 0),), REACH)[positions]

    tiles = block_tile.reshape(1, blocks)
    values = charges.reshape(flat)
    outgoing_shape = jax.ShapeDtypeStruct((slots, cell_count + 128), F32)
    outgoing = streamed(
        first_tiles,
        capacity,
        outgoing_shape,
        pl.ANY,
        held(owners, tiles, values, stencil, outgoing_shape),
        (3 + steps, 1),
        [],
        [owners, tiles, values, stencil],
    )
    swapped_edges = swap_edges(plan, *edges)
    arrived = exchange(outgoing.reshape(devices, capacity, -1)).reshape(slots, -1)
    early = swap_mirrored(plan, early)
    arrived, late, edges, couple = lax.optimization_barrier((arrived, late, edges, couple))
    late = swap_mirrored(plan, late)
    marked = arrived
    spectrum = to_columns(arrived, marked, NARROW)
    spectrum, early = lax.optimization_barrier((spectrum, early))
    own = staying_green(plan, green)
    spectrum, couple, sources, own = lax.optimization_barrier(
        (exchange(spectrum), couple, sources, own)
    )
    green_parts = [own, early, late, *edges, *swapped_edges]
    spectrum, weights = streamed(
        first_columns,
        plan,
        (spectrum_shape, green_shape),
        (pl.ANY, pl.ANY),
        [
            *held(spectrum, green_shape, both, row_twiddle),
            *column_work,
            *held(*green_parts),
        ],
        (2 * half_steps + 2 + len(green_parts), 2 * half_steps + 1),
        [origin, partner, shares],
        [spectrum, *green_parts, both, row_twiddle],
    )
    returned = to_rows(exchange(spectrum), marked)
    near = jnp.einsum("bkps,bks->bp", couple, sources, preferred_element_type=F32)
    near, target = near.reshape(flat), target.reshape(flat)
    outgoing_shape = jax.ShapeDtypeStruct((slots, cell_count), F32)
    potentials, residual, outgoing = streamed(
        middle_blocks,
        capacity,
        (
            jax.ShapeDtypeStruct(flat, F32),
            jax.ShapeDtypeStruct(flat, BF16),
            outgoing_shape,
        ),
        (pltpu.VMEM, pltpu.VMEM, pl.ANY),
        held(owners, returned, near, target, stencil, outgoing_shape),
        (4 + steps, 1),
        [],
        [owners, returned, near, target, stencil],
    )

    arrived = exchange(outgoing.reshape(devices, capacity, -1)).reshape(slots, -1)
    residual = residual.reshape(blocks, block_size)
    terms = jnp.einsum("bkps,bp->bks", couple, residual, preferred_element_type=F32)
    spectrum = exchange(to_columns(arrived, marked, NARROW))
    spectrum, terms = lax.optimization_barrier((spectrum, terms))
    spectrum = exchange(along_columns(spectrum, weights))
    extended = jnp.zeros((blocks + 2 * REACH, block_size), F32)
    extended = extended.at[positions.reshape(-1)].add(terms.reshape(-1, block_size))
    rims = jnp.concatenate([extended[:REACH], extended[blocks + REACH :]], axis=0)
    neighbour = extended_2(rims, ((AXES, 0),), REACH)
    own_part = extended[REACH : blocks + REACH]
    own_part = own_part.at[:REACH].add(neighbour[:REACH])
    own_part = own_part.at[blocks - REACH :].add(neighbour[3 * REACH :])
    returned = to_rows(spectrum, marked)
    near = own_part.reshape(flat)
    gradient = streamed(
        last_blocks,
        capacity,
        jax.ShapeDtypeStruct(flat, F32),
        pltpu.VMEM,
        held(owners, returned, near, stencil),
        (3 + steps,),
        [],
        [owners, returned, near, stencil],
    )
    return (potentials.reshape(-1), gradient.reshape(-1))


def solution(mesh):
    rows = P(AXES)
    return jax.shard_map(
        local,
        mesh=mesh,
        in_specs=(rows, rows, rows, rows, P(None, AXES), rows, rows, rows),
        out_specs=(rows, rows),
        check_vma=False,
    )
```
